256 devices in a mesh: section: 8 (over x_hi, y), dp: 32 (over z, x_lo, core).
Axes of the slice: x: 4 (x_hi: 2, x_lo: 2; x = x_hi * 2 + x_lo), y: 4, z: 8, core: 2. Of those that a mesh axis runs over, the one named last changes fastest.
Arguments:
- patches: bfloat16 [256, 16, 2048], P('dp'), may hold values from -40 to 40
- lengths: int32 [256, 16], P('dp'), may hold values from 1 to 16, 80 in all within a row
- cotangent: bfloat16 [256, 16, 2048], P('dp'), may hold values from -6 to 6
- weights: bfloat16 [2, 8, 2048, 1792], P(None, 'section', 'dp'), may hold values from -0.125 to 0.125
Outputs:
- grad_weights: float32 [2, 8, 2048, 1792], P(None, 'section', 'dp')
The draws below stay inside these ranges and needn't reach their ends.
Inputs may be any that keep to these rules, and one draw needn't show every extreme that they name: Each row is one sequence's patch lengths in bytes, summing to 80, the largest exactly 16.
All inputs are finite; a program needn't handle non-finite values.
Results may differ from the reference program's by a relative error of at most 0.035.
Values may be sent and summed in bfloat16 or wider, within the bound.
No kernel may reach another device: no remote copies, remote signals or barrier semaphores. Data moves between devices by JAX's collectives and lax.ppermute only.
A program may use at most 128 MiB of HBM per device.

```python
import math
import jax
import jax.numpy as jnp
import numpy as np
from jax import lax

D = 2048
HEADS = 16
KV_HEADS = 4
QK_DIM = 64
V_DIM = 128
PATCH = 16
QKV_WIDTH = 1792
MICRO = 8
SEQS = 256
N_SECTION = 8
N_DP = 32


def draw_patches(key, part):
    key = jax.random.fold_in(key, 11)
    key_base, key_feature, key_token = jax.random.split(key, 3)
    shape = (SEQS, PATCH, D)
    feature_scale = jnp.exp(jax.random.uniform(key_feature, (D,), jnp.float32, math.log(0.3), math.log(3.0)))
    token_scale = jnp.exp(jax.random.uniform(key_token, (SEQS, PATCH, 1), jnp.float32, math.log(0.3), math.log(3.0)))
    base = jnp.clip(jax.random.normal(key_base, shape, jnp.float32), -5.0, 5.0)
    return jnp.clip(base * feature_scale * token_scale, -40.0, 40.0).astype(jnp.bfloat16)


def level_of(key, shape, cuts, least, largest):
    factor_of = 1.0
    for dim, shards_of in cuts:
        heights = jax.random.uniform(jax.random.fold_in(jax.random.fold_in(key, 6), dim), (shards_of,), jnp.float32, least / len(cuts), largest / len(cuts))
        factor_of = factor_of * jnp.repeat(jnp.exp(heights), shape[dim] // shards_of).reshape((-1,) + (1,) * (len(shape) - 1 - dim))
    return factor_of


def profile(number_of, total, most, lean):
    portions = [(1 << 20) // math.isqrt(rank ** lean) + 1 for rank in range(2, number_of + 1)]
    rest, given = total - most - (number_of - 1), [1] * (number_of - 1)
    while rest > 0:
        free = [i for i in range(number_of - 1) if given[i] < most]
        pool, left = sum([portions[i] for i in free]), rest
        for i in free:
            addition = min(most - given[i], max(1, left * portions[i] // pool), rest)
            given[i] = given[i] + addition
            rest = rest - addition
    return np.array([most] + given)


def ragged(key, number_of, total, most, lean):
    if number_of == 2:
        one = jax.random.randint(key, (), max(1, total - most), min(most, total - 1) + 1)
        return jnp.stack([one, total - one])
    tallies = jnp.asarray(profile(number_of, total, most, lean), jnp.int32)
    couples = (number_of - 1) // 2
    giver, sink = tallies[1:1 + 2 * couples:2], tallies[2:2 + 2 * couples:2]
    margin = jnp.minimum(giver - 1, most - sink)
    shifted = jax.random.randint(jax.random.fold_in(key, 1), (couples,), 0, 1 << 20) % (margin + 1)
    tallies = tallies.at[1:1 + 2 * couples:2].set(giver - shifted).at[2:2 + 2 * couples:2].set(sink + shifted)
    return tallies[jax.random.permutation(jax.random.fold_in(key, 2), number_of)]


def scatter_about(own_key, shape, deviation, reach, shards=(), kind=jnp.bfloat16):
    level = level_of(own_key, shape, shards, -0.22, 0.18) if shards else 1.0
    entries = jax.random.normal(own_key, shape, jnp.float32) * deviation * level
    return jnp.minimum(jnp.maximum(entries, -reach), reach).astype(kind)


def setup_inputs(seed: int = 0) -> dict:
    seeds = jax.random.split(jax.random.key(seed), 5)
    return {
        "patches": draw_patches(jax.random.fold_in(seeds[4], 71), 0),
        "lengths": jax.vmap(lambda own: ragged(own, PATCH, 5 * PATCH, 16, 2))(jax.random.split(seeds[1], SEQS)).reshape((SEQS, PATCH)).astype(jnp.int32),
        "cotangent": scatter_about(seeds[2], (SEQS, PATCH, D), 1.0, 6.0, ((0, 32),)),
        "weights": scatter_about(seeds[3], (2, N_SECTION, D, QKV_WIDTH), D ** -0.5, 0.125, ((1, 8), (2, 32))),
    }


ROPE_BASE = 500000.0
EPSILON = 1e-05

def rotary_tables(lengths, half_size):
    starts = jnp.cumsum(lengths, axis=-1) - lengths
    freqs = ROPE_BASE ** (-jnp.arange(half_size, dtype=jnp.float32) * 2.0 / (2 * half_size))
    angles = starts.astype(jnp.float32)[..., None] * freqs
    return (jnp.cos(angles), jnp.sin(angles))

def normalize(widened):
    return widened * lax.rsqrt(lax.optimization_barrier(jnp.mean(widened * widened, axis=-1, keepdims=True)) + EPSILON)

def rotate(values, cosine, sine):
    half_size = values.shape[-1] // 2
    extra = (1,) * (values.ndim - 3)
    cosine_wide = cosine.reshape(cosine.shape[:2] + extra + cosine.shape[2:])
    sine_wide = sine.reshape(sine.shape[:2] + extra + sine.shape[2:])
    first_half = values[..., :half_size]
    second_half = values[..., half_size:]
    return jnp.concatenate([first_half * cosine_wide - second_half * sine_wide, first_half * sine_wide + second_half * cosine_wide], axis=-1)

def attend(packed, cosine, sine, rounding):
    seq_count = packed.shape[0]
    patch_count = packed.shape[1]
    group_size = HEADS // KV_HEADS
    query_width = HEADS * QK_DIM
    key_width = KV_HEADS * QK_DIM
    queries = packed[..., :query_width].reshape(seq_count, patch_count, KV_HEADS, group_size, QK_DIM)
    keys_part = packed[..., query_width:query_width + key_width].reshape(seq_count, patch_count, KV_HEADS, QK_DIM)
    values_part = packed[..., query_width + key_width:].reshape(seq_count, patch_count, KV_HEADS, V_DIM)
    queries = rotate(queries, cosine, sine)
    keys_part = rotate(keys_part, cosine, sine)
    scores = jnp.einsum('bqgrd,bkgd->bgrqk', queries, keys_part) / math.sqrt(QK_DIM)
    causal = jnp.tril(jnp.ones((patch_count, patch_count), jnp.float32))
    raised = jnp.exp(jnp.where(causal > 0.5, scores, 0.0)) * causal
    probs = raised / lax.optimization_barrier(jnp.sum(raised, axis=-1, keepdims=True))
    if rounding:
        probs = lax.optimization_barrier(probs.astype(jnp.bfloat16)).astype(jnp.float32)
    mixed = jnp.einsum('bgrqk,bkgv->bqgrv', probs, values_part)
    return mixed.reshape(seq_count, patch_count, HEADS * V_DIM)

def layer_forward(inputs, weight, cosine, sine):
    widened = inputs.astype(jnp.float32)
    normed = normalize(widened).astype(jnp.bfloat16)
    flat_normed = normed.reshape(-1, normed.shape[-1])
    qkv = jnp.dot(flat_normed, weight, preferred_element_type=jnp.float32).astype(jnp.bfloat16)
    qkv = qkv.reshape(inputs.shape[0], inputs.shape[1], weight.shape[1])
    mixed = attend(qkv.astype(jnp.float32), cosine, sine, True)
    return ((widened + mixed).astype(jnp.bfloat16), normed, qkv)

def layer_backward(upstream, inputs, qkv, weight, cosine, sine):
    grad_up = upstream.astype(jnp.float32)

    def plain_attend(packed):
        return attend(packed, cosine, sine, False)
    _, attend_pull = jax.vjp(plain_attend, qkv.astype(jnp.float32))
    grad_qkv = attend_pull(grad_up)[0].astype(jnp.bfloat16)
    flat_grad = grad_qkv.reshape(-1, grad_qkv.shape[-1])
    grad_normed = lax.dot_general(flat_grad, weight, (((1,), (1,)), ((), ())), preferred_element_type=jnp.float32)
    grad_normed = grad_normed.reshape(inputs.shape)
    _, norm_pull = jax.vjp(normalize, inputs.astype(jnp.float32))
    grad_inputs = norm_pull(grad_normed)[0]
    return ((grad_up + grad_inputs).astype(jnp.bfloat16), grad_qkv)

def weight_grad(normed, grad_qkv):
    group_normed = normed.reshape(N_DP, MICRO * PATCH, D)
    group_grad = grad_qkv.reshape(N_DP, MICRO * PATCH, QKV_WIDTH)

    def accumulate(total, pair):
        partial_sum = lax.dot_general(pair[0], pair[1], (((0,), (0,)), ((), ())), preferred_element_type=jnp.float32)
        rounded = lax.optimization_barrier(partial_sum.astype(jnp.bfloat16))
        return (total + rounded.astype(jnp.float32), None)
    total, _ = lax.scan(accumulate, jnp.zeros((D, QKV_WIDTH), jnp.float32), (group_normed, group_grad))
    return total

def reference(patches, lengths, cotangent, weights):
    cosine, sine = rotary_tables(lengths, QK_DIM // 2)
    layer_count = 2 * N_SECTION
    flat_weights = weights.reshape(layer_count, D, QKV_WIDTH)
    saved = []
    current = patches
    for layer in range(layer_count):
        following, normed, qkv = layer_forward(current, flat_weights[layer], cosine, sine)
        saved.append((current, normed, qkv))
        current = following
    upstream = cotangent
    grads = [None] * layer_count
    for layer in reversed(range(layer_count)):
        inputs, normed, qkv = saved[layer]
        upstream, grad_qkv = layer_backward(upstream, inputs, qkv, flat_weights[layer], cosine, sine)
        grads[layer] = weight_grad(normed, grad_qkv)
    return jnp.stack(grads).reshape(2, N_SECTION, D, QKV_WIDTH)
```

```python
import jax
import jax.numpy as jnp
from jax import lax
from jax.experimental import pallas as pl
from jax.experimental.pallas import tpu as pltpu
from jax.sharding import Mesh, PartitionSpec as P

D = 2048
HEADS = 16
KV_HEADS = 4
GROUP = HEADS // KV_HEADS
QK_DIM = 64
V_DIM = 128
PATCH = 16
QUERY_WIDTH = HEADS * QK_DIM
KEY_WIDTH = KV_HEADS * QK_DIM
VALUE_START = QUERY_WIDTH + KEY_WIDTH
WIDTH = VALUE_START + KV_HEADS * V_DIM
ROPE_BASE = 500000.0
EPSILON = 1e-05
LAYERS = 4
LANES = 128
COLUMNS = 256
STAGE_X = (0, 2, 1, 3)
F32 = jnp.float32
BF16 = jnp.bfloat16


def dot(a, b, a_dim, b_dim):
    return lax.dot_general(
        a, b, (((a_dim,), (b_dim,)), ((), ())), preferred_element_type=F32
    )


def lane_index(rows):
    return lax.broadcasted_iota(jnp.int32, (rows, LANES), 1)


def swap_halves(chunk):
    lanes = lane_index(chunk.shape[0])
    ahead = pltpu.roll(chunk, LANES - QK_DIM // 2, 1)
    behind = pltpu.roll(chunk, QK_DIM // 2, 1)
    return jnp.where(lanes % QK_DIM < QK_DIM // 2, ahead, behind)


def score_mask(tokens):
    rows = lax.broadcasted_iota(jnp.int32, (GROUP * tokens, tokens), 0) % tokens
    columns = lax.broadcasted_iota(jnp.int32, (GROUP * tokens, tokens), 1)
    return (rows // PATCH == columns // PATCH) & (columns <= rows)


def rotated_chunk(qkv, index, cosine, sine):
    chunk = qkv[:, index * LANES : (index + 1) * LANES]
    return chunk * cosine + swap_halves(chunk) * sine


def group_parts(qkv, group, cosine, sine):
    low = lane_index(qkv.shape[0]) < QK_DIM
    rows = []
    for pair in range(2):
        chunk = rotated_chunk(qkv, 2 * group + pair, cosine, sine)
        rows.append(jnp.where(low, chunk, 0.0))
        rows.append(jnp.where(low, 0.0, chunk))
    queries = jnp.concatenate(rows, axis=0).astype(BF16)
    chunk = rotated_chunk(qkv, QUERY_WIDTH // LANES + group // 2, cosine, sine)
    other = pltpu.roll(chunk, QK_DIM, 1)
    keys_part = jnp.where(low, chunk, other) if group % 2 == 0 else jnp.where(low, other, chunk)
    values_part = qkv[:, VALUE_START + group * V_DIM : VALUE_START + (group + 1) * V_DIM]
    return queries, keys_part.astype(BF16), values_part.astype(BF16)


def group_probs(queries, keys_part, mask):
    scores = dot(queries, keys_part, 1, 1) * (1.0 / QK_DIM**0.5)
    raised = jnp.where(mask, jnp.exp(jnp.where(mask, scores, 0.0)), 0.0)
    return raised / jnp.sum(raised, axis=-1, keepdims=True)


def weight_copies(layer, weights_ref, held, sems):
    copies = []
    for core in range(2):
        for low in range(2):
            copies.append(
                pltpu.make_async_copy(
                    weights_ref.at[layer, :, core, low],
                    held.at[layer, :, low, core],
                    sems.at[layer, core, low],
                )
            )
    return copies


def forward_kernel(
    x_ref, cosine_ref, sine_ref, weights_ref, last_ref, inputs_ref, normed_ref, qkv_ref,
    held, current, sems,
):
    layer = pl.program_id(0)
    tokens = x_ref.shape[0]

    @pl.when(layer == 0)
    def start():
        for each in range(LAYERS):
            for copy in weight_copies(each, weights_ref, held, sems):
                copy.start()
        current[...] = x_ref[...]

    x = current[...]
    inputs_ref[0] = x
    wide = x.astype(F32)
    scale = lax.rsqrt(jnp.mean(wide * wide, axis=-1, keepdims=True) + EPSILON)
    normed = (wide * scale).astype(BF16)
    normed_ref[0] = normed
    for copy in weight_copies(layer, weights_ref, held, sems):
        copy.wait()
    for step in range(WIDTH // COLUMNS):
        columns = slice(step * COLUMNS, (step + 1) * COLUMNS)
        block = held[layer, :, :, :, :, columns].reshape(D, COLUMNS)
        qkv_ref[0, :, columns] = dot(normed, block, 1, 0).astype(BF16)
    qkv = qkv_ref[0].astype(F32)
    cosine = cosine_ref[...]
    sine = sine_ref[...]
    mask = score_mask(tokens)
    for group in range(KV_HEADS):
        queries, keys_part, values_part = group_parts(qkv, group, cosine, sine)
        probs = group_probs(queries, keys_part, mask).astype(BF16)
        mixed = dot(probs, values_part, 1, 0)
        for r in range(GROUP):
            head = group * GROUP + r
            span = slice(head * V_DIM, (head + 1) * V_DIM)
            current[:, span] = (
                x[:, span].astype(F32) + mixed[r * tokens : (r + 1) * tokens]
            ).astype(BF16)

    @pl.when(layer == LAYERS - 1)
    def finish():
        last_ref[...] = current[...]


def backward_kernel(
    g_ref, cosine_ref, sine_ref, inputs_ref, qkv_ref, weights_ref, first_ref, grad_ref,
    held, current, sems,
):
    step = pl.program_id(0)
    layer = LAYERS - 1 - step
    tokens = g_ref.shape[0]

    @pl.when(step == 0)
    def start():
        for each in reversed(range(LAYERS)):
            for copy in weight_copies(each, weights_ref, held, sems):
                copy.start()
        current[...] = g_ref[...]

    upstream = current[...]
    cosine = cosine_ref[...]
    sine = sine_ref[...]
    mask = score_mask(tokens)
    low = lane_index(tokens) < QK_DIM
    qkv = qkv_ref[0].astype(F32)
    key_grads = []
    for group in range(KV_HEADS):
        queries, keys_part, values_part = group_parts(qkv, group, cosine, sine)
        probs = group_probs(queries, keys_part, mask)
        rows = [
            upstream[:, (group * GROUP + r) * V_DIM : (group * GROUP + r + 1) * V_DIM]
            for r in range(GROUP)
        ]
        stacked = jnp.concatenate(rows, axis=0)
        grad_probs = dot(stacked, values_part, 1, 1)
        weighted = jnp.sum(probs * grad_probs, axis=-1, keepdims=True)
        grad_scores = (probs * (grad_probs - weighted) * (1.0 / QK_DIM**0.5)).astype(BF16)
        grad_values = dot(probs.astype(BF16), stacked, 0, 0)
        grad_ref[0, :, VALUE_START + group * V_DIM : VALUE_START + (group + 1) * V_DIM] = (
            grad_values.astype(BF16)
        )
        grad_queries = dot(grad_scores, keys_part, 1, 0)
        for pair in range(2):
            first = grad_queries[2 * pair * tokens : (2 * pair + 1) * tokens]
            second = grad_queries[(2 * pair + 1) * tokens : (2 * pair + 2) * tokens]
            chunk = jnp.where(low, first, second)
            chunk = chunk * cosine - swap_halves(chunk) * sine
            start_at = (2 * group + pair) * LANES
            grad_ref[0, :, start_at : start_at + LANES] = chunk.astype(BF16)
        halves = dot(grad_scores, queries, 0, 0)
        key_grads.append(halves + pltpu.roll(halves, QK_DIM, 1))
    for pair in range(2):
        chunk = jnp.where(low, key_grads[2 * pair], key_grads[2 * pair + 1])
        chunk = chunk * cosine - swap_halves(chunk) * sine
        start_at = QUERY_WIDTH + pair * LANES
        grad_ref[0, :, start_at : start_at + LANES] = chunk.astype(BF16)
    for copy in weight_copies(layer, weights_ref, held, sems):
        copy.wait()
    grad_qkv = grad_ref[0]
    wide = inputs_ref[0].astype(F32)
    parts = []
    for z in range(D // COLUMNS):
        block = held[layer, z].reshape(COLUMNS, WIDTH)
        parts.append(dot(grad_qkv, block, 1, 1))
    grad_normed = jnp.concatenate(parts, axis=1)
    scale = lax.rsqrt(jnp.mean(wide * wide, axis=-1, keepdims=True) + EPSILON)
    inner = jnp.mean(grad_normed * wide, axis=-1, keepdims=True)
    grad_inputs = scale * grad_normed - wide * (scale * scale * scale * inner)
    current[...] = (upstream.astype(F32) + grad_inputs).astype(BF16)

    @pl.when(step == LAYERS - 1)
    def finish():
        first_ref[...] = current[...]


def whole(shape):
    return pl.BlockSpec(shape, lambda i: (0,) * len(shape))


def scratches(tokens):
    return [
        pltpu.VMEM((LAYERS, 8, 2, 2, 64, WIDTH), BF16),
        pltpu.VMEM((tokens, D), BF16),
        pltpu.SemaphoreType.DMA((LAYERS, 2, 2)),
    ]


PARAMS = dict(vmem_limit_bytes=52 * 1024 * 1024)


def run_forward(x, cosine, sine, weights):
    tokens = x.shape[0]
    per_layer = lambda width: pl.BlockSpec((1, tokens, width), lambda i: (i, 0, 0))
    return pl.pallas_call(
        forward_kernel,
        grid=(LAYERS,),
        in_specs=[
            whole((tokens, D)),
            whole((tokens, LANES)),
            whole((tokens, LANES)),
            pl.BlockSpec(memory_space=pl.ANY),
        ],
        out_specs=[whole((tokens, D)), per_layer(D), per_layer(D), per_layer(WIDTH)],
        out_shape=[
            jax.ShapeDtypeStruct((tokens, D), BF16),
            jax.ShapeDtypeStruct((LAYERS, tokens, D), BF16),
            jax.ShapeDtypeStruct((LAYERS, tokens, D), BF16),
            jax.ShapeDtypeStruct((LAYERS, tokens, WIDTH), BF16),
        ],
        scratch_shapes=scratches(tokens),
        compiler_params=pltpu.CompilerParams(**PARAMS),
        cost_estimate=pl.CostEstimate(
            flops=2 * LAYERS * tokens * D * WIDTH,
            bytes_accessed=2 * LAYERS * D * WIDTH,
            transcendentals=0,
        ),
        name="forward_stage",
    )(x, cosine, sine, weights)


def run_backward(g, cosine, sine, inputs, qkv, weights):
    tokens = g.shape[0]
    per_layer = lambda width: pl.BlockSpec((1, tokens, width), lambda i: (LAYERS - 1 - i, 0, 0))
    return pl.pallas_call(
        backward_kernel,
        grid=(LAYERS,),
        in_specs=[
            whole((tokens, D)),
            whole((tokens, LANES)),
            whole((tokens, LANES)),
            per_layer(D),
            per_layer(WIDTH),
            pl.BlockSpec(memory_space=pl.ANY),
        ],
        out_specs=[whole((tokens, D)), per_layer(WIDTH)],
        out_shape=[
            jax.ShapeDtypeStruct((tokens, D), BF16),
            jax.ShapeDtypeStruct((LAYERS, tokens, WIDTH), BF16),
        ],
        scratch_shapes=scratches(tokens),
        compiler_params=pltpu.CompilerParams(**PARAMS),
        cost_estimate=pl.CostEstimate(
            flops=2 * LAYERS * tokens * D * WIDTH,
            bytes_accessed=2 * LAYERS * D * WIDTH,
            transcendentals=0,
        ),
        name="backward_stage",
    )(g, cosine, sine, inputs, qkv, weights)


def ring(size, by):
    return [(i, (i + by) % size) for i in range(size)]


def from_partner(value):
    return lax.ppermute(value, "xl", ring(2, 1))


def both_halves(value, low_x):
    other = from_partner(value)
    return jnp.where(low_x == 0, jnp.stack([value, other]), jnp.stack([other, value]))


def rotary_tables(lengths):
    half = QK_DIM // 2
    starts = jnp.cumsum(lengths, axis=-1) - lengths
    freqs = ROPE_BASE ** (-jnp.arange(half, dtype=F32) * 2.0 / (2 * half))
    angles = starts.astype(F32).reshape(-1, 1) * freqs
    cosine, sine = jnp.cos(angles), jnp.sin(angles)
    return (
        jnp.concatenate([cosine] * 4, axis=1),
        jnp.concatenate([-sine, sine, -sine, sine], axis=1),
    )


def spread_over_y(value, place):
    pieces = [lax.dynamic_index_in_dim(value, place, 0, keepdims=False)]
    for by in (1, 3, 2):
        piece = lax.dynamic_index_in_dim(value, (place + by) % 4, 0, keepdims=False)
        pieces.append(lax.ppermute(piece, "y", ring(4, by)))
    return pieces


def local(patches, lengths, cotangent, weights):
    high_x = lax.axis_index("xh")
    low_x = lax.axis_index("xl")
    place = lax.axis_index("y")
    core = lax.axis_index("core")
    stage = high_x + 2 * low_x
    rows = weights.shape[2]

    own = lax.dynamic_index_in_dim(weights, low_x, 0, keepdims=False)[0]
    partner_own = lax.dynamic_index_in_dim(weights, 1 - low_x, 0, keepdims=False)[0]
    other = from_partner(partner_own)
    shard = jnp.where(low_x == 0, jnp.stack([own, other]), jnp.stack([other, own]))
    gathered = lax.all_gather(shard, ("y", "z", "core"), axis=0, tiled=False)
    gathered = gathered.reshape(LAYERS, 8, 2, 2, rows, WIDTH)

    pick = lambda v: lax.dynamic_slice_in_dim(v, 2 * place, 2, 0)
    tokens = 4 * PATCH
    x = both_halves(pick(patches).reshape(2 * PATCH, D), low_x).reshape(tokens, D)
    g = both_halves(pick(cotangent).reshape(2 * PATCH, D), low_x).reshape(tokens, D)
    span = both_halves(pick(lengths).astype(F32), low_x).reshape(4, PATCH).astype(jnp.int32)
    cosine, sine = rotary_tables(span)

    stored = (
        jnp.zeros((LAYERS, tokens, D), BF16),
        jnp.zeros((LAYERS, tokens, D), BF16),
        jnp.zeros((LAYERS, tokens, WIDTH), BF16),
    )
    for turn in range(LAYERS):
        if turn > 0:
            x = lax.ppermute(x, ("xh", "xl"), [(STAGE_X[turn - 1], STAGE_X[turn])])

        def active(x, stored):
            last, inputs, normed, qkv = run_forward(x, cosine, sine, gathered)
            return last, (inputs, normed, qkv)

        x, stored = lax.cond(stage == turn, active, lambda x, s: (x, s), x, stored)
    inputs, normed, qkv = stored

    grads = jnp.zeros((LAYERS, tokens, WIDTH), BF16)
    for turn in reversed(range(LAYERS)):
        if turn < LAYERS - 1:
            g = lax.ppermute(g, ("xh", "xl"), [(STAGE_X[turn + 1], STAGE_X[turn])])

        def active(g, grads):
            return tuple(run_backward(g, cosine, sine, inputs, qkv, gathered))

        g, grads = lax.cond(stage == turn, active, lambda g, s: (g, s), g, grads)

    normed_rows = jnp.concatenate(spread_over_y(normed, place))
    sibling = lambda v: lax.ppermute(v, "core", ring(2, 1))
    normed_rows = jnp.concatenate([normed_rows, sibling(normed_rows)])
    half = WIDTH // 2
    grad_rows = jnp.concatenate(spread_over_y(grads, place))
    mine = lax.dynamic_slice_in_dim(grad_rows, core * half, half, 1)
    sent = lax.dynamic_slice_in_dim(grad_rows, (1 - core) * half, half, 1)
    grad_rows = jnp.concatenate([mine, sibling(sent)])
    terms = dot(normed_rows, grad_rows, 0, 0).astype(BF16)
    total = lax.psum_scatter(terms, "z", scatter_dimension=0, tiled=True)
    total = total.reshape(2, 2, rows, half)
    mine = lax.dynamic_index_in_dim(total, core, 1, keepdims=False)
    received = sibling(lax.dynamic_index_in_dim(total, 1 - core, 1, keepdims=False))
    total = jnp.where(
        core == 0,
        jnp.concatenate([mine, received], axis=2),
        jnp.concatenate([received, mine], axis=2),
    )
    kept = lax.dynamic_index_in_dim(total, low_x, 0, keepdims=False)
    swapped = from_partner(lax.dynamic_index_in_dim(total, 1 - low_x, 0, keepdims=False))
    result = jnp.where(low_x == 0, jnp.stack([kept, swapped]), jnp.stack([swapped, kept]))
    return result.astype(F32)[:, None]


def solution(mesh):
    fine = Mesh(mesh.devices.reshape(2, 4, 8, 2, 2), ("xh", "y", "z", "xl", "core"))
    dp = ("z", "xl", "core")
    return jax.shard_map(
        local,
        mesh=fine,
        in_specs=(
            P(dp, None, None),
            P(dp, None),
            P(dp, None, None),
            P(None, ("xh", "y"), dp, None),
        ),
        out_specs=P(None, ("xh", "y"), dp, None),
        check_vma=False,
    )
```

```python
import jax
import jax.numpy as jnp
from jax import lax
from jax.experimental import pallas as pl
from jax.experimental.pallas import tpu as pltpu
from jax.sharding import Mesh, PartitionSpec as P

D = 2048
HEADS = 16
KV_HEADS = 4
GROUP = HEADS // KV_HEADS
QK_DIM = 64
V_DIM = 128
PATCH = 16
QUERY_WIDTH = HEADS * QK_DIM
KEY_WIDTH = KV_HEADS * QK_DIM
VALUE_START = QUERY_WIDTH + KEY_WIDTH
WIDTH = VALUE_START + KV_HEADS * V_DIM
ROPE_BASE = 500000.0
EPSILON = 1e-05
LAYERS = 4
LANES = 128
COLUMNS = 256
STAGE_X = (0, 2, 1, 3)
F32 = jnp.float32
BF16 = jnp.bfloat16


def dot(a, b, a_dim, b_dim):
    return lax.dot_general(
        a, b, (((a_dim,), (b_dim,)), ((), ())), preferred_element_type=F32
    )


def lane_index(rows):
    return lax.broadcasted_iota(jnp.int32, (rows, LANES), 1)


def swap_halves(chunk):
    lanes = lane_index(chunk.shape[0])
    ahead = pltpu.roll(chunk, LANES - QK_DIM // 2, 1)
    behind = pltpu.roll(chunk, QK_DIM // 2, 1)
    return jnp.where(lanes % QK_DIM < QK_DIM // 2, ahead, behind)


def score_mask(tokens):
    rows = lax.broadcasted_iota(jnp.int32, (GROUP * tokens, tokens), 0) % tokens
    columns = lax.broadcasted_iota(jnp.int32, (GROUP * tokens, tokens), 1)
    return (rows // PATCH == columns // PATCH) & (columns <= rows)


def rotated_chunk(qkv, index, cosine, sine):
    chunk = qkv[:, index * LANES : (index + 1) * LANES]
    return chunk * cosine + swap_halves(chunk) * sine


def group_parts(qkv, group, cosine, sine):
    low = lane_index(qkv.shape[0]) < QK_DIM
    rows = []
    for pair in range(2):
        chunk = rotated_chunk(qkv, 2 * group + pair, cosine, sine)
        rows.append(jnp.where(low, chunk, 0.0))
        rows.append(jnp.where(low, 0.0, chunk))
    queries = jnp.concatenate(rows, axis=0).astype(BF16)
    chunk = rotated_chunk(qkv, QUERY_WIDTH // LANES + group // 2, cosine, sine)
    other = pltpu.roll(chunk, QK_DIM, 1)
    keys_part = jnp.where(low, chunk, other) if group % 2 == 0 else jnp.where(low, other, chunk)
    values_part = qkv[:, VALUE_START + group * V_DIM : VALUE_START + (group + 1) * V_DIM]
    return queries, keys_part.astype(BF16), values_part.astype(BF16)


def group_probs(queries, keys_part, mask):
    scores = dot(queries, keys_part, 1, 1) * (1.0 / QK_DIM**0.5)
    raised = jnp.where(mask, jnp.exp(jnp.where(mask, scores, 0.0)), 0.0)
    return raised / jnp.sum(raised, axis=-1, keepdims=True)


def column_copies(slot, layer, step, weights_ref, held, sems):
    columns = pl.ds(step * COLUMNS, COLUMNS)
    return [
        pltpu.make_async_copy(
            weights_ref.at[layer, :, core, low, :, columns],
            held.at[slot, :, low, core, :, columns],
            sems.at[slot, step, core, low],
        )
        for core in range(2)
        for low in range(2)
    ]


def row_copies(slot, layer, step, weights_ref, held, sems):
    return [
        pltpu.make_async_copy(
            weights_ref.at[layer, step, core, low],
            held.at[slot, step, low, core],
            sems.at[slot, step, core, low],
        )
        for core in range(2)
        for low in range(2)
    ]


def start_all(copies):
    for copy in copies:
        copy.start()


def wait_all(copies):
    for copy in copies:
        copy.wait()


COLUMN_STEPS = WIDTH // COLUMNS
ROW_STEPS = D // COLUMNS
AHEAD = 5


def forward_layer(
    layer, final, cosine, sine, mask, weights_ref,
    inputs_ref, normed_ref, values_ref, queries_ref, keys_ref, probs_ref, target,
    held, qkv_ref, sems,
):
    x = inputs_ref[layer]
    tokens = x.shape[0]
    slot = layer % 2
    wide = x.astype(F32)
    scale = lax.rsqrt(jnp.mean(wide * wide, axis=-1, keepdims=True) + EPSILON)
    normed = (wide * scale).astype(BF16)
    normed_ref[layer] = normed
    for step in range(COLUMN_STEPS):
        wait_all(column_copies(slot, layer, step, weights_ref, held, sems))
        later = step + AHEAD
        if later < COLUMN_STEPS:
            start_all(column_copies(slot, layer, later, weights_ref, held, sems))
        elif not final:
            later -= COLUMN_STEPS
            start_all(column_copies(1 - slot, layer + 1, later, weights_ref, held, sems))
        columns = slice(step * COLUMNS, (step + 1) * COLUMNS)
        block = held[slot, :, :, :, :, columns].reshape(D, COLUMNS)
        qkv_ref[:, columns] = dot(normed, block, 1, 0).astype(BF16)
    qkv = qkv_ref[...].astype(F32)
    values_ref[layer] = qkv_ref[:, VALUE_START:]
    for group in range(KV_HEADS):
        queries, keys_part, values_part = group_parts(qkv, group, cosine, sine)
        probs = group_probs(queries, keys_part, mask)
        queries_ref[layer, group] = queries
        keys_ref[layer, group] = keys_part
        probs_ref[layer, group] = probs
        mixed = dot(probs.astype(BF16), values_part, 1, 0)
        for r in range(GROUP):
            head = group * GROUP + r
            span = slice(head * V_DIM, (head + 1) * V_DIM)
            value = inputs_ref[layer, :, span].astype(F32) + mixed[r * tokens : (r + 1) * tokens]
            target(span, value.astype(BF16))


def store_copies(layer, local_refs, outer_refs, sems, inward):
    copies = []
    for index, (inner, outer) in enumerate(zip(local_refs, outer_refs)):
        ends = (outer.at[layer], inner.at[layer]) if inward else (inner.at[layer], outer.at[layer])
        copies.append(pltpu.make_async_copy(*ends, sems.at[layer, index]))
    return copies


def forward_kernel(flag_ref, x_ref, cosine_ref, sine_ref, weights_ref, *rest):
    held, qkv_ref, *stores, sems, out_sems = rest[-10:]
    last_ref, *outs = rest[-17:-10]
    inputs_ref = stores[0]

    @pl.when(flag_ref[0] == 1)
    def active():
        for step in range(AHEAD):
            start_all(column_copies(0, 0, step, weights_ref, held, sems))
        inputs_ref[0] = x_ref[...]
        cosine = cosine_ref[...]
        sine = sine_ref[...]
        mask = score_mask(x_ref.shape[0])

        def run(layer, final, target):
            forward_layer(
                layer, final, cosine, sine, mask, weights_ref, *stores, target,
                held, qkv_ref, sems,
            )
            start_all(store_copies(layer, stores, outs, out_sems, False))

        def body(layer, carry):
            def target(span, value):
                inputs_ref[layer + 1, :, span] = value

            run(layer, False, target)
            return carry

        lax.fori_loop(0, LAYERS - 1, body, 0)

        def target(span, value):
            last_ref[:, span] = value

        run(LAYERS - 1, True, target)
        for layer in range(LAYERS):
            wait_all(store_copies(layer, stores, outs, out_sems, False))


def backward_layer(
    layer, final, cosine_ref, sine_ref, weights_ref, inputs_ref, values_ref, queries_ref,
    keys_ref, probs_ref, first_ref, grad_ref, held, sems,
):
    upstream = first_ref[...]
    tokens = upstream.shape[0]
    slot = layer % 2
    cosine = cosine_ref[...]
    sine = sine_ref[...]
    low = lane_index(tokens) < QK_DIM
    key_grads = []
    for group in range(KV_HEADS):
        queries = queries_ref[layer, group]
        keys_part = keys_ref[layer, group]
        probs = probs_ref[layer, group]
        values_part = values_ref[layer, :, group * V_DIM : (group + 1) * V_DIM]
        rows = [
            upstream[:, (group * GROUP + r) * V_DIM : (group * GROUP + r + 1) * V_DIM]
            for r in range(GROUP)
        ]
        stacked = jnp.concatenate(rows, axis=0)
        grad_probs = dot(stacked, values_part, 1, 1)
        weighted = jnp.sum(probs * grad_probs, axis=-1, keepdims=True)
        grad_scores = (probs * (grad_probs - weighted) * (1.0 / QK_DIM**0.5)).astype(BF16)
        grad_values = dot(probs.astype(BF16), stacked, 0, 0)
        grad_ref[layer, :, VALUE_START + group * V_DIM : VALUE_START + (group + 1) * V_DIM] = (
            grad_values.astype(BF16)
        )
        grad_queries = dot(grad_scores, keys_part, 1, 0)
        for pair in range(2):
            first = grad_queries[2 * pair * tokens : (2 * pair + 1) * tokens]
            second = grad_queries[(2 * pair + 1) * tokens : (2 * pair + 2) * tokens]
            chunk = jnp.where(low, first, second)
            chunk = chunk * cosine - swap_halves(chunk) * sine
            start_at = (2 * group + pair) * LANES
            grad_ref[layer, :, start_at : start_at + LANES] = chunk.astype(BF16)
        halves = dot(grad_scores, queries, 0, 0)
        key_grads.append(halves + pltpu.roll(halves, QK_DIM, 1))
    for pair in range(2):
        chunk = jnp.where(low, key_grads[2 * pair], key_grads[2 * pair + 1])
        chunk = chunk * cosine - swap_halves(chunk) * sine
        start_at = QUERY_WIDTH + pair * LANES
        grad_ref[layer, :, start_at : start_at + LANES] = chunk.astype(BF16)
    grad_qkv = grad_ref[layer]
    wide = inputs_ref[layer].astype(F32)
    parts = []
    for step in range(ROW_STEPS):
        wait_all(row_copies(slot, layer, step, weights_ref, held, sems))
        if not final:
            start_all(row_copies(1 - slot, layer - 1, step, weights_ref, held, sems))
        block = held[slot, step].reshape(COLUMNS, WIDTH)
        parts.append(dot(grad_qkv, block, 1, 1))
    grad_normed = jnp.concatenate(parts, axis=1)
    scale = lax.rsqrt(jnp.mean(wide * wide, axis=-1, keepdims=True) + EPSILON)
    inner = jnp.mean(grad_normed * wide, axis=-1, keepdims=True)
    grad_inputs = scale * grad_normed - wide * (scale * scale * scale * inner)
    first_ref[...] = (upstream.astype(F32) + grad_inputs).astype(BF16)


def backward_kernel(flag_ref, g_ref, cosine_ref, sine_ref, weights_ref, *rest):
    outer = rest[:5]
    first_ref, grad_out, held, *stores, grad_ref, sems, in_sems, out_sems = rest[-12:]

    @pl.when(flag_ref[0] == 1)
    def active():
        top = LAYERS - 1
        start_all(store_copies(top, stores, outer, in_sems, True))
        for step in range(ROW_STEPS):
            start_all(row_copies(top % 2, top, step, weights_ref, held, sems))
        for layer in reversed(range(top)):
            start_all(store_copies(layer, stores, outer, in_sems, True))
        first_ref[...] = g_ref[...]

        def run(layer, final):
            wait_all(store_copies(layer, stores, outer, in_sems, True))
            backward_layer(
                layer, final, cosine_ref, sine_ref, weights_ref, *stores, first_ref, grad_ref,
                held, sems,
            )
            start_all(store_copies(layer, [grad_ref], [grad_out], out_sems, False))

        def body(step, carry):
            run(top - step, False)
            return carry

        lax.fori_loop(0, top, body, 0)
        run(0, True)
        for layer in range(LAYERS):
            wait_all(store_copies(layer, [grad_ref], [grad_out], out_sems, False))


VMEM_SPEC = pl.BlockSpec(memory_space=pltpu.VMEM)
SMEM_SPEC = pl.BlockSpec(memory_space=pltpu.SMEM)
HBM_SPEC = pl.BlockSpec(memory_space=pltpu.HBM)
STAGE_PARAMS = pltpu.CompilerParams(vmem_limit_bytes=34 * 1024 * 1024)


def stage_cost(tokens):
    return pl.CostEstimate(
        flops=2 * LAYERS * tokens * D * WIDTH,
        bytes_accessed=2 * LAYERS * D * WIDTH,
        transcendentals=0,
    )


def buffers(shapes):
    return [pltpu.VMEM(each.shape, each.dtype) for each in shapes]


HELD = pltpu.VMEM((2, 8, 2, 2, 64, WIDTH), BF16)
WEIGHT_SEMS = pltpu.SemaphoreType.DMA((2, ROW_STEPS, 2, 2))


def copy_sems(count):
    return pltpu.SemaphoreType.DMA((LAYERS, count))


def store_shapes(tokens):
    return [
        jax.ShapeDtypeStruct((LAYERS, tokens, D), BF16),
        jax.ShapeDtypeStruct((LAYERS, tokens, D), BF16),
        jax.ShapeDtypeStruct((LAYERS, tokens, KV_HEADS * V_DIM), BF16),
        jax.ShapeDtypeStruct((LAYERS, KV_HEADS, GROUP * tokens, LANES), BF16),
        jax.ShapeDtypeStruct((LAYERS, KV_HEADS, tokens, LANES), BF16),
        jax.ShapeDtypeStruct((LAYERS, KV_HEADS, GROUP * tokens, tokens), F32),
    ]


def in_hbm(value):
    return pltpu.with_memory_space_constraint(value, pltpu.HBM)


def in_hbm_shape(shape):
    return pltpu.HBM(shape.shape, shape.dtype)


def grad_shape(tokens):
    return jax.ShapeDtypeStruct((LAYERS, tokens, WIDTH), BF16)


def run_forward(flag, x, cosine, sine, weights, stored):
    tokens = x.shape[0]
    shapes = store_shapes(tokens)
    return pl.pallas_call(
        forward_kernel,
        in_specs=[SMEM_SPEC] + [VMEM_SPEC] * 3 + [HBM_SPEC] * (1 + len(stored)),
        out_specs=[VMEM_SPEC] + [HBM_SPEC] * len(shapes),
        out_shape=[jax.ShapeDtypeStruct((tokens, D), BF16), *map(in_hbm_shape, shapes)],
        input_output_aliases={5 + i: 1 + i for i in range(len(stored))},
        scratch_shapes=[
            HELD,
            pltpu.VMEM((tokens, WIDTH), BF16),
            *buffers(shapes),
            WEIGHT_SEMS,
            copy_sems(len(shapes)),
        ],
        cost_estimate=stage_cost(tokens),
        name="forward_stage",
        compiler_params=STAGE_PARAMS,
    )(flag, x, cosine, sine, *map(in_hbm, [weights, *stored]))


def run_backward(flag, g, cosine, sine, weights, stored, grads):
    tokens = g.shape[0]
    shapes = store_shapes(tokens)
    return pl.pallas_call(
        backward_kernel,
        in_specs=[SMEM_SPEC] + [VMEM_SPEC] * 3 + [HBM_SPEC] * (6 + len(grads)),
        out_specs=[VMEM_SPEC, HBM_SPEC],
        out_shape=[jax.ShapeDtypeStruct((tokens, D), BF16), in_hbm_shape(grad_shape(tokens))],
        input_output_aliases={10: 1} if grads else {},
        scratch_shapes=[
            HELD,
            *buffers([shapes[0], *shapes[2:], grad_shape(tokens)]),
            WEIGHT_SEMS,
            copy_sems(5),
            copy_sems(1),
        ],
        cost_estimate=stage_cost(tokens),
        name="backward_stage",
        compiler_params=STAGE_PARAMS,
    )(flag, g, cosine, sine, *map(in_hbm, [weights, *stored, *grads]))


def ring(size, by):
    return [(i, (i + by) % size) for i in range(size)]


def from_partner(value):
    return lax.ppermute(value, "xl", ring(2, 1))


def both_halves(value, low_x):
    other = from_partner(value)
    return jnp.where(low_x == 0, jnp.stack([value, other]), jnp.stack([other, value]))


def rotary_tables(lengths):
    half = QK_DIM // 2
    starts = jnp.cumsum(lengths, axis=-1) - lengths
    freqs = ROPE_BASE ** (-jnp.arange(half, dtype=F32) * 2.0 / (2 * half))
    angles = starts.astype(F32).reshape(-1, 1) * freqs
    cosine, sine = jnp.cos(angles), jnp.sin(angles)
    return (
        jnp.concatenate([cosine] * 4, axis=1),
        jnp.concatenate([-sine, sine, -sine, sine], axis=1),
    )


def spread_over_y(value, place):
    pieces = [lax.dynamic_index_in_dim(value, place, 0, keepdims=False)]
    for by in (1, 3, 2):
        piece = lax.dynamic_index_in_dim(value, (place + by) % 4, 0, keepdims=False)
        pieces.append(lax.ppermute(piece, "y", ring(4, by)))
    return pieces


def local(patches, lengths, cotangent, weights):
    high_x = lax.axis_index("xh")
    low_x = lax.axis_index("xl")
    place = lax.axis_index("y")
    core = lax.axis_index("core")
    stage = high_x + 2 * low_x
    rows = weights.shape[2]

    own = lax.dynamic_index_in_dim(weights, low_x, 0, keepdims=False)[0]
    partner_own = lax.dynamic_index_in_dim(weights, 1 - low_x, 0, keepdims=False)[0]
    other = from_partner(partner_own)
    shard = jnp.where(low_x == 0, jnp.stack([own, other]), jnp.stack([other, own]))
    gathered = lax.all_gather(shard, ("y", "z", "core"), axis=0, tiled=False)
    gathered = gathered.reshape(LAYERS, 8, 2, 2, rows, WIDTH)

    pick = lambda v: lax.dynamic_slice_in_dim(v, 2 * place, 2, 0)
    tokens = 4 * PATCH
    x = both_halves(pick(patches).reshape(2 * PATCH, D), low_x).reshape(tokens, D)
    g = both_halves(pick(cotangent).reshape(2 * PATCH, D), low_x).reshape(tokens, D)
    span = both_halves(pick(lengths).astype(F32), low_x).reshape(4, PATCH).astype(jnp.int32)
    cosine, sine = rotary_tables(span)

    stored = []
    for turn in range(LAYERS):
        flag = (stage == turn).astype(jnp.int32).reshape(1)
        if turn > 0:
            x = lax.ppermute(x, ("xh", "xl"), [(STAGE_X[turn - 1], STAGE_X[turn])])
        x, *stored = run_forward(flag, x, cosine, sine, gathered, stored)
    inputs, normed, *shared = stored

    grads = []
    for turn in reversed(range(LAYERS)):
        flag = (stage == turn).astype(jnp.int32).reshape(1)
        if turn < LAYERS - 1:
            g = lax.ppermute(g, ("xh", "xl"), [(STAGE_X[turn + 1], STAGE_X[turn])])
        g, *grads = run_backward(flag, g, cosine, sine, gathered, [inputs, *shared], grads)
    grads = grads[0]

    normed_rows = jnp.concatenate(spread_over_y(normed, place))
    sibling = lambda v: lax.ppermute(v, "core", ring(2, 1))
    normed_rows = jnp.concatenate([normed_rows, sibling(normed_rows)])
    half = WIDTH // 2
    grad_rows = jnp.concatenate(spread_over_y(grads, place))
    mine = lax.dynamic_slice_in_dim(grad_rows, core * half, half, 1)
    sent = lax.dynamic_slice_in_dim(grad_rows, (1 - core) * half, half, 1)
    grad_rows = jnp.concatenate([mine, sibling(sent)])
    terms = dot(normed_rows, grad_rows, 0, 0).astype(BF16)
    total = lax.psum_scatter(terms, "z", scatter_dimension=0, tiled=True)
    total = total.reshape(2, 2, rows, half)

    def block(low, row_core):
        return lax.dynamic_slice(total, (low, row_core, 0, 0), (1, 1, rows, half))[0, 0]

    came = [[block(low_x, core), None], [None, None]]
    for far in range(2):
        for beside in range(2):
            if far or beside:
                pairs = [(i, i ^ (2 * far + beside)) for i in range(4)]
                came[far][beside] = lax.ppermute(
                    block(low_x ^ far, core ^ beside), ("xl", "core"), pairs
                )

    def source(low, col):
        same_core = [jnp.where(core == col, came[far][0], came[far][1]) for far in range(2)]
        return jnp.where(low_x == low, same_core[0], same_core[1])

    result = jnp.stack(
        [jnp.concatenate([source(low, col) for col in range(2)], axis=1) for low in range(2)]
    )
    return result.astype(F32)[:, None]


def solution(mesh):
    fine = Mesh(mesh.devices.reshape(2, 4, 8, 2, 2), ("xh", "y", "z", "xl", "core"))
    dp = ("z", "xl", "core")
    return jax.shard_map(
        local,
        mesh=fine,
        in_specs=(
            P(dp, None, None),
            P(dp, None),
            P(dp, None, None),
            P(None, ("xh", "y"), dp, None),
        ),
        out_specs=P(None, ("xh", "y"), dp, None),
        check_vma=False,
    )
```

```python
import jax
import jax.numpy as jnp
from jax import lax
from jax.experimental import pallas as pl
from jax.experimental.pallas import tpu as pltpu
from jax.sharding import Mesh, PartitionSpec as P

D = 2048
HEADS = 16
KV_HEADS = 4
GROUP = HEADS // KV_HEADS
QK_DIM = 64
V_DIM = 128
PATCH = 16
QUERY_WIDTH = HEADS * QK_DIM
KEY_WIDTH = KV_HEADS * QK_DIM
VALUE_START = QUERY_WIDTH + KEY_WIDTH
WIDTH = VALUE_START + KV_HEADS * V_DIM
ROPE_BASE = 500000.0
EPSILON = 1e-05
LAYERS = 4
LANES = 128
COLUMNS = 256
STAGE_X = (0, 2, 1, 3)
F32 = jnp.float32
BF16 = jnp.bfloat16


def dot(a, b, a_dim, b_dim):
    return lax.dot_general(
        a, b, (((a_dim,), (b_dim,)), ((), ())), preferred_element_type=F32
    )


def lane_index(rows):
    return lax.broadcasted_iota(jnp.int32, (rows, LANES), 1)


def swap_halves(chunk):
    lanes = lane_index(chunk.shape[0])
    ahead = pltpu.roll(chunk, LANES - QK_DIM // 2, 1)
    behind = pltpu.roll(chunk, QK_DIM // 2, 1)
    return jnp.where(lanes % QK_DIM < QK_DIM // 2, ahead, behind)


def score_mask(tokens):
    rows = lax.broadcasted_iota(jnp.int32, (GROUP * tokens, tokens), 0) % tokens
    columns = lax.broadcasted_iota(jnp.int32, (GROUP * tokens, tokens), 1)
    return (rows // PATCH == columns // PATCH) & (columns <= rows)


def rotated_chunk(qkv, index, cosine, sine):
    chunk = qkv[:, index * LANES : (index + 1) * LANES]
    return chunk * cosine + swap_halves(chunk) * sine


def group_parts(qkv, group, cosine, sine):
    low = lane_index(qkv.shape[0]) < QK_DIM
    rows = []
    for pair in range(2):
        chunk = rotated_chunk(qkv, 2 * group + pair, cosine, sine)
        rows.append(jnp.where(low, chunk, 0.0))
        rows.append(jnp.where(low, 0.0, chunk))
    queries = jnp.concatenate(rows, axis=0).astype(BF16)
    chunk = rotated_chunk(qkv, QUERY_WIDTH // LANES + group // 2, cosine, sine)
    other = pltpu.roll(chunk, QK_DIM, 1)
    keys_part = jnp.where(low, chunk, other) if group % 2 == 0 else jnp.where(low, other, chunk)
    values_part = qkv[:, VALUE_START + group * V_DIM : VALUE_START + (group + 1) * V_DIM]
    return queries, keys_part.astype(BF16), values_part.astype(BF16)


def group_probs(queries, keys_part, mask):
    scores = dot(queries, keys_part, 1, 1) * (1.0 / QK_DIM**0.5)
    raised = jnp.where(mask, jnp.exp(jnp.where(mask, scores, 0.0)), 0.0)
    return raised / jnp.sum(raised, axis=-1, keepdims=True)


def layer_copies(slot, layer, weights_ref, held, sems):
    return [
        pltpu.make_async_copy(
            weights_ref.at[layer, :, core, low], held.at[slot, :, low, core], sems.at[slot, core, low]
        )
        for core in range(2)
        for low in range(2)
    ]


def start_all(copies):
    for copy in copies:
        copy.start()


def wait_all(copies):
    for copy in copies:
        copy.wait()


COLUMN_STEPS = WIDTH // COLUMNS
ROW_STEPS = D // COLUMNS
SLOTS = LAYERS - 1


def forward_layer(
    layer, ready, block_of, cosine, sine, mask,
    inputs_ref, normed_ref, values_ref, queries_ref, keys_ref, probs_ref, target, qkv_ref,
):
    x = inputs_ref[layer]
    tokens = x.shape[0]
    wide = x.astype(F32)
    scale = lax.rsqrt(jnp.mean(wide * wide, axis=-1, keepdims=True) + EPSILON)
    normed = (wide * scale).astype(BF16)
    normed_ref[layer] = normed
    ready()
    for step in range(COLUMN_STEPS):
        columns = slice(step * COLUMNS, (step + 1) * COLUMNS)
        block = block_of(columns).reshape(D, COLUMNS)
        qkv_ref[:, columns] = dot(normed, block, 1, 0).astype(BF16)
    qkv = qkv_ref[...].astype(F32)
    values_ref[layer] = qkv_ref[:, VALUE_START:]
    for group in range(KV_HEADS):
        queries, keys_part, values_part = group_parts(qkv, group, cosine, sine)
        probs = group_probs(queries, keys_part, mask)
        queries_ref[layer, group] = queries
        keys_ref[layer, group] = keys_part
        probs_ref[layer, group] = probs
        mixed = dot(probs.astype(BF16), values_part, 1, 0)
        for r in range(GROUP):
            head = group * GROUP + r
            span = slice(head * V_DIM, (head + 1) * V_DIM)
            value = inputs_ref[layer, :, span].astype(F32) + mixed[r * tokens : (r + 1) * tokens]
            target(span, value.astype(BF16))


def store_copies(layer, local_refs, outer_refs, sems, inward):
    copies = []
    for index, (inner, outer) in enumerate(zip(local_refs, outer_refs)):
        ends = (outer.at[layer], inner.at[layer]) if inward else (inner.at[layer], outer.at[layer])
        copies.append(pltpu.make_async_copy(*ends, sems.at[layer, index]))
    return copies


def forward_kernel(flag_ref, x_ref, cosine_ref, sine_ref, weights_ref, *rest):
    held, qkv_ref, *stores, sems, out_sems = rest[-10:]
    last_ref, *outs = rest[-17:-10]
    inputs_ref = stores[0]

    @pl.when(flag_ref[0] == 1)
    def active():
        for layer in range(LAYERS):
            start_all(layer_copies(layer, layer, weights_ref, held, sems))
        inputs_ref[0] = x_ref[...]
        cosine = cosine_ref[...]
        sine = sine_ref[...]
        mask = score_mask(x_ref.shape[0])

        def run(layer, ready, block_of, target):
            forward_layer(
                layer, ready, block_of, cosine, sine, mask, *stores, target, qkv_ref
            )
            start_all(store_copies(layer, stores, outs, out_sems, False))

        def onward(layer):
            def target(span, value):
                inputs_ref[layer + 1, :, span] = value

            return target

        def leave(span, value):
            last_ref[:, span] = value

        def held_layer(layer, target):
            run(
                layer,
                lambda: wait_all(layer_copies(layer, layer, weights_ref, held, sems)),
                lambda columns: held[layer, :, :, :, :, columns],
                target,
            )


        def body(layer, carry):
            held_layer(layer, onward(layer))
            return carry

        lax.fori_loop(0, LAYERS - 1, body, 0)
        held_layer(LAYERS - 1, leave)
        for layer in range(LAYERS):
            wait_all(store_copies(layer, stores, outs, out_sems, False))


def backward_layer(
    layer, ready, block_of, cosine_ref, sine_ref, inputs_ref, values_ref, queries_ref,
    keys_ref, probs_ref, first_ref, grad_ref,
):
    upstream = first_ref[...]
    tokens = upstream.shape[0]
    cosine = cosine_ref[...]
    sine = sine_ref[...]
    low = lane_index(tokens) < QK_DIM
    key_grads = []
    for group in range(KV_HEADS):
        queries = queries_ref[layer, group]
        keys_part = keys_ref[layer, group]
        probs = probs_ref[layer, group]
        values_part = values_ref[layer, :, group * V_DIM : (group + 1) * V_DIM]
        rows = [
            upstream[:, (group * GROUP + r) * V_DIM : (group * GROUP + r + 1) * V_DIM]
            for r in range(GROUP)
        ]
        stacked = jnp.concatenate(rows, axis=0)
        grad_probs = dot(stacked, values_part, 1, 1)
        weighted = jnp.sum(probs * grad_probs, axis=-1, keepdims=True)
        grad_scores = (probs * (grad_probs - weighted) * (1.0 / QK_DIM**0.5)).astype(BF16)
        grad_values = dot(probs.astype(BF16), stacked, 0, 0)
        grad_ref[layer, :, VALUE_START + group * V_DIM : VALUE_START + (group + 1) * V_DIM] = (
            grad_values.astype(BF16)
        )
        grad_queries = dot(grad_scores, keys_part, 1, 0)
        for pair in range(2):
            first = grad_queries[2 * pair * tokens : (2 * pair + 1) * tokens]
            second = grad_queries[(2 * pair + 1) * tokens : (2 * pair + 2) * tokens]
            chunk = jnp.where(low, first, second)
            chunk = chunk * cosine - swap_halves(chunk) * sine
            start_at = (2 * group + pair) * LANES
            grad_ref[layer, :, start_at : start_at + LANES] = chunk.astype(BF16)
        halves = dot(grad_scores, queries, 0, 0)
        key_grads.append(halves + pltpu.roll(halves, QK_DIM, 1))
    for pair in range(2):
        chunk = jnp.where(low, key_grads[2 * pair], key_grads[2 * pair + 1])
        chunk = chunk * cosine - swap_halves(chunk) * sine
        start_at = QUERY_WIDTH + pair * LANES
        grad_ref[layer, :, start_at : start_at + LANES] = chunk.astype(BF16)
    grad_qkv = grad_ref[layer]
    wide = inputs_ref[layer].astype(F32)
    parts = []
    ready()
    for step in range(ROW_STEPS):
        block = block_of(step).reshape(COLUMNS, WIDTH)
        parts.append(dot(grad_qkv, block, 1, 1))
    grad_normed = jnp.concatenate(parts, axis=1)
    scale = lax.rsqrt(jnp.mean(wide * wide, axis=-1, keepdims=True) + EPSILON)
    inner = jnp.mean(grad_normed * wide, axis=-1, keepdims=True)
    grad_inputs = scale * grad_normed - wide * (scale * scale * scale * inner)
    first_ref[...] = (upstream.astype(F32) + grad_inputs).astype(BF16)


def backward_kernel(flag_ref, g_ref, cosine_ref, sine_ref, top_ref, weights_ref, *rest):
    outer = rest[:5]
    first_ref, grad_out, held, *stores, grad_ref, sems, in_sems, out_sems = rest[-12:]

    @pl.when(flag_ref[0] == 1)
    def active():
        top = LAYERS - 1
        for layer in reversed(range(LAYERS)):
            start_all(store_copies(layer, stores, outer, in_sems, True))
            if layer < top:
                start_all(layer_copies(layer, layer, weights_ref, held, sems))
        first_ref[...] = g_ref[...]

        def run(layer, ready, block_of):
            wait_all(store_copies(layer, stores, outer, in_sems, True))
            backward_layer(
                layer, ready, block_of, cosine_ref, sine_ref, *stores, first_ref, grad_ref
            )
            start_all(store_copies(layer, [grad_ref], [grad_out], out_sems, False))

        run(top, lambda: None, lambda step: top_ref[step])

        def body(step, carry):
            layer = top - step
            run(
                layer,
                lambda: wait_all(layer_copies(layer, layer, weights_ref, held, sems)),
                lambda part: held[layer, part],
            )
            return carry

        lax.fori_loop(1, LAYERS, body, 0)
        for layer in range(LAYERS):
            wait_all(store_copies(layer, [grad_ref], [grad_out], out_sems, False))


VMEM_SPEC = pl.BlockSpec(memory_space=pltpu.VMEM)
SMEM_SPEC = pl.BlockSpec(memory_space=pltpu.SMEM)
HBM_SPEC = pl.BlockSpec(memory_space=pltpu.HBM)


def stage_params(limit):
    return pltpu.CompilerParams(vmem_limit_bytes=limit * 1024 * 1024)


def stage_cost(tokens):
    return pl.CostEstimate(
        flops=2 * LAYERS * tokens * D * WIDTH,
        bytes_accessed=2 * LAYERS * D * WIDTH,
        transcendentals=0,
    )


def buffers(shapes):
    return [pltpu.VMEM(each.shape, each.dtype) for each in shapes]


def held_scratch(slots):
    return pltpu.VMEM((slots, 8, 2, 2, 64, WIDTH), BF16)


def weight_sems(slots):
    return pltpu.SemaphoreType.DMA((slots, 2, 2))


def copy_sems(count):
    return pltpu.SemaphoreType.DMA((LAYERS, count))


def store_shapes(tokens):
    return [
        jax.ShapeDtypeStruct((LAYERS, tokens, D), BF16),
        jax.ShapeDtypeStruct((LAYERS, tokens, D), BF16),
        jax.ShapeDtypeStruct((LAYERS, tokens, KV_HEADS * V_DIM), BF16),
        jax.ShapeDtypeStruct((LAYERS, KV_HEADS, GROUP * tokens, LANES), BF16),
        jax.ShapeDtypeStruct((LAYERS, KV_HEADS, tokens, LANES), BF16),
        jax.ShapeDtypeStruct((LAYERS, KV_HEADS, GROUP * tokens, tokens), F32),
    ]


def in_hbm(value):
    return pltpu.with_memory_space_constraint(value, pltpu.HBM)


def in_hbm_shape(shape):
    return pltpu.HBM(shape.shape, shape.dtype)


def grad_shape(tokens):
    return jax.ShapeDtypeStruct((LAYERS, tokens, WIDTH), BF16)


def run_forward(flag, x, cosine, sine, weights, stored):
    tokens = x.shape[0]
    shapes = store_shapes(tokens)
    return pl.pallas_call(
        forward_kernel,
        in_specs=[SMEM_SPEC] + [VMEM_SPEC] * 3 + [HBM_SPEC] * (1 + len(stored)),
        out_specs=[VMEM_SPEC] + [HBM_SPEC] * len(shapes),
        out_shape=[jax.ShapeDtypeStruct((tokens, D), BF16), *map(in_hbm_shape, shapes)],
        input_output_aliases={5 + i: 1 + i for i in range(len(stored))},
        scratch_shapes=[
            held_scratch(LAYERS),
            pltpu.VMEM((tokens, WIDTH), BF16),
            *buffers(shapes),
            weight_sems(LAYERS),
            copy_sems(len(shapes)),
        ],
        cost_estimate=stage_cost(tokens),
        name="forward_stage",
        compiler_params=stage_params(40),
    )(flag, x, cosine, sine, *map(in_hbm, [weights, *stored]))


def run_backward(flag, g, cosine, sine, top, weights, stored, grads):
    tokens = g.shape[0]
    shapes = store_shapes(tokens)
    return pl.pallas_call(
        backward_kernel,
        in_specs=[SMEM_SPEC] + [VMEM_SPEC] * 4 + [HBM_SPEC] * (6 + len(grads)),
        out_specs=[VMEM_SPEC, HBM_SPEC],
        out_shape=[jax.ShapeDtypeStruct((tokens, D), BF16), in_hbm_shape(grad_shape(tokens))],
        input_output_aliases={11: 1} if grads else {},
        scratch_shapes=[
            held_scratch(SLOTS),
            *buffers([shapes[0], *shapes[2:], grad_shape(tokens)]),
            weight_sems(SLOTS),
            copy_sems(5),
            copy_sems(1),
        ],
        cost_estimate=stage_cost(tokens),
        name="backward_stage",
        compiler_params=stage_params(32),
    )(flag, g, cosine, sine, top, *map(in_hbm, [weights, *stored, *grads]))


def ring(size, by):
    return [(i, (i + by) % size) for i in range(size)]


def from_partner(value):
    return lax.ppermute(value, "xl", ring(2, 1))


def both_halves(value, low_x):
    other = from_partner(value)
    return jnp.where(low_x == 0, jnp.stack([value, other]), jnp.stack([other, value]))


def rotary_tables(lengths):
    half = QK_DIM // 2
    starts = jnp.cumsum(lengths, axis=-1) - lengths
    freqs = ROPE_BASE ** (-jnp.arange(half, dtype=F32) * 2.0 / (2 * half))
    angles = starts.astype(F32).reshape(-1, 1) * freqs
    cosine, sine = jnp.cos(angles), jnp.sin(angles)
    return (
        jnp.concatenate([cosine] * 4, axis=1),
        jnp.concatenate([-sine, sine, -sine, sine], axis=1),
    )


def ordered(gathered, layer):
    return jnp.swapaxes(gathered[layer], 1, 2)


def spread_over_y(value, place):
    pieces = [lax.dynamic_index_in_dim(value, place, 0, keepdims=False)]
    for by in (1, 3, 2):
        piece = lax.dynamic_index_in_dim(value, (place + by) % 4, 0, keepdims=False)
        pieces.append(lax.ppermute(piece, "y", ring(4, by)))
    return pieces


def local(patches, lengths, cotangent, weights):
    high_x = lax.axis_index("xh")
    low_x = lax.axis_index("xl")
    place = lax.axis_index("y")
    core = lax.axis_index("core")
    stage = high_x + 2 * low_x
    rows = weights.shape[2]

    own = lax.dynamic_index_in_dim(weights, low_x, 0, keepdims=False)[0]
    partner_own = lax.dynamic_index_in_dim(weights, 1 - low_x, 0, keepdims=False)[0]
    other = from_partner(partner_own)
    shard = jnp.where(low_x == 0, jnp.stack([own, other]), jnp.stack([other, own]))
    gathered = lax.all_gather(shard, ("y", "z", "core"), axis=0, tiled=False)
    gathered = gathered.reshape(LAYERS, 8, 2, 2, rows, WIDTH)

    pick = lambda v: lax.dynamic_slice_in_dim(v, 2 * place, 2, 0)
    tokens = 4 * PATCH
    x = both_halves(pick(patches).reshape(2 * PATCH, D), low_x).reshape(tokens, D)
    g = both_halves(pick(cotangent).reshape(2 * PATCH, D), low_x).reshape(tokens, D)
    span = both_halves(pick(lengths).astype(F32), low_x).reshape(4, PATCH).astype(jnp.int32)
    cosine, sine = rotary_tables(span)

    stored = []
    for turn in range(LAYERS):
        flag = (stage == turn).astype(jnp.int32).reshape(1)
        if turn > 0:
            x = lax.ppermute(x, ("xh", "xl"), [(STAGE_X[turn - 1], STAGE_X[turn])])
        x, *stored = run_forward(flag, x, cosine, sine, gathered, stored)
        if turn == 0:
            x, late = lax.optimization_barrier((x, gathered))
            top = ordered(late, LAYERS - 1)
    inputs, normed, *shared = stored

    grads = []
    for turn in reversed(range(LAYERS)):
        flag = (stage == turn).astype(jnp.int32).reshape(1)
        if turn < LAYERS - 1:
            g = lax.ppermute(g, ("xh", "xl"), [(STAGE_X[turn + 1], STAGE_X[turn])])
        g, *grads = run_backward(flag, g, cosine, sine, top, gathered, [inputs, *shared], grads)
    grads = grads[0]

    normed_rows = jnp.concatenate(spread_over_y(normed, place))
    sibling = lambda v: lax.ppermute(v, "core", ring(2, 1))
    normed_rows = jnp.concatenate([normed_rows, sibling(normed_rows)])
    half = WIDTH // 2
    grad_rows = jnp.concatenate(spread_over_y(grads, place))
    mine = lax.dynamic_slice_in_dim(grad_rows, core * half, half, 1)
    sent = lax.dynamic_slice_in_dim(grad_rows, (1 - core) * half, half, 1)
    grad_rows = jnp.concatenate([mine, sibling(sent)])
    terms = dot(normed_rows, grad_rows, 0, 0).astype(BF16)
    total = lax.psum_scatter(terms, "z", scatter_dimension=0, tiled=True)
    total = total.reshape(2, 2, rows, half)

    def block(low, row_core):
        return lax.dynamic_slice(total, (low, row_core, 0, 0), (1, 1, rows, half))[0, 0]

    came = [[block(low_x, core), None], [None, None]]
    for far in range(2):
        for beside in range(2):
            if far or beside:
                pairs = [(i, i ^ (2 * far + beside)) for i in range(4)]
                came[far][beside] = lax.ppermute(
                    block(low_x ^ far, core ^ beside), ("xl", "core"), pairs
                )

    def source(low, col):
        same_core = [jnp.where(core == col, came[far][0], came[far][1]) for far in range(2)]
        return jnp.where(low_x == low, same_core[0], same_core[1])

    result = jnp.stack(
        [jnp.concatenate([source(low, col) for col in range(2)], axis=1) for low in range(2)]
    )
    return result.astype(F32)[:, None]


def solution(mesh):
    fine = Mesh(mesh.devices.reshape(2, 4, 8, 2, 2), ("xh", "y", "z", "xl", "core"))
    dp = ("z", "xl", "core")
    return jax.shard_map(
        local,
        mesh=fine,
        in_specs=(
            P(dp, None, None),
            P(dp, None),
            P(dp, None, None),
            P(None, ("xh", "y"), dp, None),
        ),
        out_specs=P(None, ("xh", "y"), dp, None),
        check_vma=False,
    )
```

```python
import jax
import jax.numpy as jnp
from jax import lax
from jax.experimental import pallas as pl
from jax.experimental.pallas import tpu as pltpu
from jax.sharding import Mesh, PartitionSpec as P

D = 2048
HEADS = 16
KV_HEADS = 4
GROUP = HEADS // KV_HEADS
QK_DIM = 64
V_DIM = 128
PATCH = 16
QUERY_WIDTH = HEADS * QK_DIM
KEY_WIDTH = KV_HEADS * QK_DIM
VALUE_START = QUERY_WIDTH + KEY_WIDTH
WIDTH = VALUE_START + KV_HEADS * V_DIM
ROPE_BASE = 500000.0
EPSILON = 1e-05
LAYERS = 4
LANES = 128
COLUMNS = 256
STAGE_X = (0, 2, 1, 3)
F32 = jnp.float32
BF16 = jnp.bfloat16


def dot(a, b, a_dim, b_dim):
    return lax.dot_general(
        a, b, (((a_dim,), (b_dim,)), ((), ())), preferred_element_type=F32
    )


def lane_index(rows):
    return lax.broadcasted_iota(jnp.int32, (rows, LANES), 1)


def swap_halves(chunk):
    lanes = lane_index(chunk.shape[0])
    ahead = pltpu.roll(chunk, LANES - QK_DIM // 2, 1)
    behind = pltpu.roll(chunk, QK_DIM // 2, 1)
    return jnp.where(lanes % QK_DIM < QK_DIM // 2, ahead, behind)


def score_mask(tokens):
    rows = lax.broadcasted_iota(jnp.int32, (GROUP * tokens, tokens), 0) % tokens
    columns = lax.broadcasted_iota(jnp.int32, (GROUP * tokens, tokens), 1)
    return (rows // PATCH == columns // PATCH) & (columns <= rows)


def rotated_chunk(qkv, index, cosine, sine):
    chunk = qkv[:, index * LANES : (index + 1) * LANES]
    return chunk * cosine + swap_halves(chunk) * sine


def group_parts(qkv, group, cosine, sine):
    low = lane_index(qkv.shape[0]) < QK_DIM
    rows = []
    for pair in range(2):
        chunk = rotated_chunk(qkv, 2 * group + pair, cosine, sine)
        rows.append(jnp.where(low, chunk, 0.0))
        rows.append(jnp.where(low, 0.0, chunk))
    queries = jnp.concatenate(rows, axis=0).astype(BF16)
    chunk = rotated_chunk(qkv, QUERY_WIDTH // LANES + group // 2, cosine, sine)
    other = pltpu.roll(chunk, QK_DIM, 1)
    keys_part = jnp.where(low, chunk, other) if group % 2 == 0 else jnp.where(low, other, chunk)
    values_part = qkv[:, VALUE_START + group * V_DIM : VALUE_START + (group + 1) * V_DIM]
    return queries, keys_part.astype(BF16), values_part.astype(BF16)


def group_probs(queries, keys_part, mask):
    scores = dot(queries, keys_part, 1, 1) * (1.0 / QK_DIM**0.5)
    raised = jnp.where(mask, jnp.exp(jnp.where(mask, scores, 0.0)), 0.0)
    return raised / jnp.sum(raised, axis=-1, keepdims=True)


def layer_copies(slot, layer, weights_ref, held, sems):
    return [
        pltpu.make_async_copy(
            weights_ref.at[layer, :, core, low], held.at[slot, :, low, core], sems.at[slot, core, low]
        )
        for core in range(2)
        for low in range(2)
    ]


def start_all(copies):
    for copy in copies:
        copy.start()


def wait_all(copies):
    for copy in copies:
        copy.wait()


COLUMN_STEPS = WIDTH // COLUMNS
ROW_STEPS = D // COLUMNS
SLOTS = LAYERS - 1


def forward_layer(
    layer, ready, block_of, cosine, sine, mask,
    inputs_ref, normed_ref, values_ref, queries_ref, keys_ref, probs_ref, target, qkv_ref,
):
    x = inputs_ref[layer]
    tokens = x.shape[0]
    wide = x.astype(F32)
    scale = lax.rsqrt(jnp.mean(wide * wide, axis=-1, keepdims=True) + EPSILON)
    normed = (wide * scale).astype(BF16)
    normed_ref[layer] = normed
    ready()
    for step in range(COLUMN_STEPS):
        columns = slice(step * COLUMNS, (step + 1) * COLUMNS)
        block = block_of(columns).reshape(D, COLUMNS)
        qkv_ref[:, columns] = dot(normed, block, 1, 0).astype(BF16)
    qkv = qkv_ref[...].astype(F32)
    values_ref[layer] = qkv_ref[:, VALUE_START:]
    for group in range(KV_HEADS):
        queries, keys_part, values_part = group_parts(qkv, group, cosine, sine)
        probs = group_probs(queries, keys_part, mask)
        queries_ref[layer, group] = queries
        keys_ref[layer, group] = keys_part
        probs_ref[layer, group] = probs
        mixed = dot(probs.astype(BF16), values_part, 1, 0)
        for r in range(GROUP):
            head = group * GROUP + r
            span = slice(head * V_DIM, (head + 1) * V_DIM)
            value = inputs_ref[layer, :, span].astype(F32) + mixed[r * tokens : (r + 1) * tokens]
            target(span, value.astype(BF16))


def store_copies(layer, local_refs, outer_refs, sems, inward):
    copies = []
    for index, (inner, outer) in enumerate(zip(local_refs, outer_refs)):
        ends = (outer.at[layer], inner.at[layer]) if inward else (inner.at[layer], outer.at[layer])
        copies.append(pltpu.make_async_copy(*ends, sems.at[layer, index]))
    return copies


def forward_stage(
    x_ref, cosine_ref, sine_ref, weights_ref, stores, outs, held, qkv_ref, sems, out_sems, leave
):
    inputs_ref = stores[0]
    for layer in range(LAYERS):
        start_all(layer_copies(layer, layer, weights_ref, held, sems))
    inputs_ref[0] = x_ref[...]
    cosine = cosine_ref[...]
    sine = sine_ref[...]
    mask = score_mask(x_ref.shape[0])

    def run(layer, target):
        forward_layer(
            layer,
            lambda: wait_all(layer_copies(layer, layer, weights_ref, held, sems)),
            lambda columns: held[layer, :, :, :, :, columns],
            cosine, sine, mask, *stores, target, qkv_ref,
        )
        start_all(store_copies(layer, stores[: len(outs)], outs, out_sems, False))

    def body(layer, carry):
        def target(span, value):
            inputs_ref[layer + 1, :, span] = value

        run(layer, target)
        return carry

    lax.fori_loop(0, LAYERS - 1, body, 0)
    run(LAYERS - 1, leave)


def forward_kernel(flag_ref, x_ref, cosine_ref, sine_ref, weights_ref, *rest):
    held, qkv_ref, *stores, sems, out_sems = rest[-10:]
    last_ref, *outs = rest[-17:-10]

    @pl.when(flag_ref[0] == 1)
    def active():
        def leave(span, value):
            last_ref[:, span] = value

        forward_stage(
            x_ref, cosine_ref, sine_ref, weights_ref, stores, outs, held, qkv_ref, sems,
            out_sems, leave,
        )
        for layer in range(LAYERS):
            wait_all(store_copies(layer, stores, outs, out_sems, False))


def turn_kernel(flag_ref, x_ref, g_ref, cosine_ref, sine_ref, weights_ref, _normed, *rest):
    first_ref, normed_out, grad_out, held, qkv_ref, *stores = rest[:-4]
    grad_ref, sems, out_sems, grad_sems = rest[-4:]
    normed_ref, inputs_ref, *shared = stores

    @pl.when(flag_ref[0] == 1)
    def active():
        def leave(span, value):
            first_ref[:, span] = value

        forward_stage(
            x_ref, cosine_ref, sine_ref, weights_ref, [inputs_ref, normed_ref, *shared], [],
            held, qkv_ref, sems, out_sems, leave,
        )
        for layer in range(LAYERS):
            start_all(store_copies(layer, [normed_ref], [normed_out], out_sems, False))
        first_ref[...] = g_ref[...]

        def body(step, carry):
            layer = LAYERS - 1 - step
            backward_layer(
                layer, lambda: None, lambda part: held[layer, part], cosine_ref, sine_ref,
                inputs_ref, *shared, first_ref, grad_ref,
            )
            start_all(store_copies(layer, [grad_ref], [grad_out], grad_sems, False))
            return carry

        lax.fori_loop(0, LAYERS, body, 0)
        for layer in range(LAYERS):
            wait_all(store_copies(layer, [normed_ref], [normed_out], out_sems, False))
            wait_all(store_copies(layer, [grad_ref], [grad_out], grad_sems, False))


def backward_layer(
    layer, ready, block_of, cosine_ref, sine_ref, inputs_ref, values_ref, queries_ref,
    keys_ref, probs_ref, first_ref, grad_ref,
):
    upstream = first_ref[...]
    tokens = upstream.shape[0]
    cosine = cosine_ref[...]
    sine = sine_ref[...]
    low = lane_index(tokens) < QK_DIM
    key_grads = []
    for group in range(KV_HEADS):
        queries = queries_ref[layer, group]
        keys_part = keys_ref[layer, group]
        probs = probs_ref[layer, group]
        values_part = values_ref[layer, :, group * V_DIM : (group + 1) * V_DIM]
        rows = [
            upstream[:, (group * GROUP + r) * V_DIM : (group * GROUP + r + 1) * V_DIM]
            for r in range(GROUP)
        ]
        stacked = jnp.concatenate(rows, axis=0)
        grad_probs = dot(stacked, values_part, 1, 1)
        weighted = jnp.sum(probs * grad_probs, axis=-1, keepdims=True)
        grad_scores = (probs * (grad_probs - weighted) * (1.0 / QK_DIM**0.5)).astype(BF16)
        grad_values = dot(probs.astype(BF16), stacked, 0, 0)
        grad_ref[layer, :, VALUE_START + group * V_DIM : VALUE_START + (group + 1) * V_DIM] = (
            grad_values.astype(BF16)
        )
        grad_queries = dot(grad_scores, keys_part, 1, 0)
        for pair in range(2):
            first = grad_queries[2 * pair * tokens : (2 * pair + 1) * tokens]
            second = grad_queries[(2 * pair + 1) * tokens : (2 * pair + 2) * tokens]
            chunk = jnp.where(low, first, second)
            chunk = chunk * cosine - swap_halves(chunk) * sine
            start_at = (2 * group + pair) * LANES
            grad_ref[layer, :, start_at : start_at + LANES] = chunk.astype(BF16)
        halves = dot(grad_scores, queries, 0, 0)
        key_grads.append(halves + pltpu.roll(halves, QK_DIM, 1))
    for pair in range(2):
        chunk = jnp.where(low, key_grads[2 * pair], key_grads[2 * pair + 1])
        chunk = chunk * cosine - swap_halves(chunk) * sine
        start_at = QUERY_WIDTH + pair * LANES
        grad_ref[layer, :, start_at : start_at + LANES] = chunk.astype(BF16)
    grad_qkv = grad_ref[layer]
    wide = inputs_ref[layer].astype(F32)
    parts = []
    ready()
    for step in range(ROW_STEPS):
        block = block_of(step).reshape(COLUMNS, WIDTH)
        parts.append(dot(grad_qkv, block, 1, 1))
    grad_normed = jnp.concatenate(parts, axis=1)
    scale = lax.rsqrt(jnp.mean(wide * wide, axis=-1, keepdims=True) + EPSILON)
    inner = jnp.mean(grad_normed * wide, axis=-1, keepdims=True)
    grad_inputs = scale * grad_normed - wide * (scale * scale * scale * inner)
    first_ref[...] = (upstream.astype(F32) + grad_inputs).astype(BF16)


def backward_kernel(flag_ref, g_ref, cosine_ref, sine_ref, top_ref, weights_ref, *rest):
    outer = rest[:5]
    first_ref, grad_out, held, *stores, grad_ref, sems, in_sems, out_sems = rest[-12:]

    @pl.when(flag_ref[0] == 1)
    def active():
        top = LAYERS - 1
        for layer in reversed(range(LAYERS)):
            start_all(store_copies(layer, stores, outer, in_sems, True))
            if layer < top:
                start_all(layer_copies(layer, layer, weights_ref, held, sems))
        first_ref[...] = g_ref[...]

        def run(layer, ready, block_of):
            wait_all(store_copies(layer, stores, outer, in_sems, True))
            backward_layer(
                layer, ready, block_of, cosine_ref, sine_ref, *stores, first_ref, grad_ref
            )
            start_all(store_copies(layer, [grad_ref], [grad_out], out_sems, False))

        run(top, lambda: None, lambda step: top_ref[step])

        def body(step, carry):
            layer = top - step
            run(
                layer,
                lambda: wait_all(layer_copies(layer, layer, weights_ref, held, sems)),
                lambda part: held[layer, part],
            )
            return carry

        lax.fori_loop(1, LAYERS, body, 0)
        for layer in range(LAYERS):
            wait_all(store_copies(layer, [grad_ref], [grad_out], out_sems, False))


VMEM_SPEC = pl.BlockSpec(memory_space=pltpu.VMEM)
SMEM_SPEC = pl.BlockSpec(memory_space=pltpu.SMEM)
HBM_SPEC = pl.BlockSpec(memory_space=pltpu.HBM)


def stage_params(limit):
    return pltpu.CompilerParams(vmem_limit_bytes=limit * 1024 * 1024)


def stage_cost(tokens):
    return pl.CostEstimate(
        flops=2 * LAYERS * tokens * D * WIDTH,
        bytes_accessed=2 * LAYERS * D * WIDTH,
        transcendentals=0,
    )


def buffers(shapes):
    return [pltpu.VMEM(each.shape, each.dtype) for each in shapes]


def held_scratch(slots):
    return pltpu.VMEM((slots, 8, 2, 2, 64, WIDTH), BF16)


def weight_sems(slots):
    return pltpu.SemaphoreType.DMA((slots, 2, 2))


def copy_sems(count):
    return pltpu.SemaphoreType.DMA((LAYERS, count))


def store_shapes(tokens):
    return [
        jax.ShapeDtypeStruct((LAYERS, tokens, D), BF16),
        jax.ShapeDtypeStruct((LAYERS, tokens, D), BF16),
        jax.ShapeDtypeStruct((LAYERS, tokens, KV_HEADS * V_DIM), BF16),
        jax.ShapeDtypeStruct((LAYERS, KV_HEADS, GROUP * tokens, LANES), BF16),
        jax.ShapeDtypeStruct((LAYERS, KV_HEADS, tokens, LANES), BF16),
        jax.ShapeDtypeStruct((LAYERS, KV_HEADS, GROUP * tokens, tokens), F32),
    ]


def in_hbm(value):
    return pltpu.with_memory_space_constraint(value, pltpu.HBM)


def in_hbm_shape(shape):
    return pltpu.HBM(shape.shape, shape.dtype)


def grad_shape(tokens):
    return jax.ShapeDtypeStruct((LAYERS, tokens, WIDTH), BF16)


def run_forward(flag, x, cosine, sine, weights, stored):
    tokens = x.shape[0]
    shapes = store_shapes(tokens)
    return pl.pallas_call(
        forward_kernel,
        in_specs=[SMEM_SPEC] + [VMEM_SPEC] * 3 + [HBM_SPEC] * (1 + len(stored)),
        out_specs=[VMEM_SPEC] + [HBM_SPEC] * len(shapes),
        out_shape=[jax.ShapeDtypeStruct((tokens, D), BF16), *map(in_hbm_shape, shapes)],
        input_output_aliases={5 + i: 1 + i for i in range(len(stored))},
        scratch_shapes=[
            held_scratch(LAYERS),
            pltpu.VMEM((tokens, WIDTH), BF16),
            *buffers(shapes),
            weight_sems(LAYERS),
            copy_sems(len(shapes)),
        ],
        cost_estimate=stage_cost(tokens),
        name="forward_stage",
        compiler_params=stage_params(40),
    )(flag, x, cosine, sine, *map(in_hbm, [weights, *stored]))


def run_turn(flag, x, g, cosine, sine, weights, normed):
    tokens = g.shape[0]
    shapes = store_shapes(tokens)
    return pl.pallas_call(
        turn_kernel,
        in_specs=[SMEM_SPEC] + [VMEM_SPEC] * 4 + [HBM_SPEC] * 2,
        out_specs=[VMEM_SPEC] + [HBM_SPEC] * 2,
        out_shape=[
            jax.ShapeDtypeStruct((tokens, D), BF16),
            in_hbm_shape(shapes[1]),
            in_hbm_shape(grad_shape(tokens)),
        ],
        input_output_aliases={6: 1},
        scratch_shapes=[
            held_scratch(LAYERS),
            pltpu.VMEM((tokens, WIDTH), BF16),
            *buffers([shapes[1], shapes[0], *shapes[2:]]),
            pltpu.VMEM((LAYERS, tokens, WIDTH), BF16),
            weight_sems(LAYERS),
            copy_sems(1),
            copy_sems(1),
        ],
        cost_estimate=stage_cost(tokens),
        name="turn_stage",
        compiler_params=stage_params(42),
    )(flag, x, g, cosine, sine, *map(in_hbm, [weights, normed]))


def run_backward(flag, g, cosine, sine, top, weights, stored, grads):
    tokens = g.shape[0]
    shapes = store_shapes(tokens)
    return pl.pallas_call(
        backward_kernel,
        in_specs=[SMEM_SPEC] + [VMEM_SPEC] * 4 + [HBM_SPEC] * (6 + len(grads)),
        out_specs=[VMEM_SPEC, HBM_SPEC],
        out_shape=[jax.ShapeDtypeStruct((tokens, D), BF16), in_hbm_shape(grad_shape(tokens))],
        input_output_aliases={11: 1} if grads else {},
        scratch_shapes=[
            held_scratch(SLOTS),
            *buffers([shapes[0], *shapes[2:], grad_shape(tokens)]),
            weight_sems(SLOTS),
            copy_sems(5),
            copy_sems(1),
        ],
        cost_estimate=stage_cost(tokens),
        name="backward_stage",
        compiler_params=stage_params(32),
    )(flag, g, cosine, sine, top, *map(in_hbm, [weights, *stored, *grads]))


def ring(size, by):
    return [(i, (i + by) % size) for i in range(size)]


def from_partner(value):
    return lax.ppermute(value, "xl", ring(2, 1))


def both_halves(value, low_x):
    other = from_partner(value)
    return jnp.where(low_x == 0, jnp.stack([value, other]), jnp.stack([other, value]))


def rotary_tables(lengths):
    half = QK_DIM // 2
    starts = jnp.cumsum(lengths, axis=-1) - lengths
    freqs = ROPE_BASE ** (-jnp.arange(half, dtype=F32) * 2.0 / (2 * half))
    angles = starts.astype(F32).reshape(-1, 1) * freqs
    cosine, sine = jnp.cos(angles), jnp.sin(angles)
    return (
        jnp.concatenate([cosine] * 4, axis=1),
        jnp.concatenate([-sine, sine, -sine, sine], axis=1),
    )


def ordered(gathered, layer):
    return jnp.swapaxes(gathered[layer], 1, 2)


def spread_over_y(value, place):
    pieces = [lax.dynamic_index_in_dim(value, place, 0, keepdims=False)]
    for by in (1, 3, 2):
        piece = lax.dynamic_index_in_dim(value, (place + by) % 4, 0, keepdims=False)
        pieces.append(lax.ppermute(piece, "y", ring(4, by)))
    return pieces


def local(patches, lengths, cotangent, weights):
    high_x = lax.axis_index("xh")
    low_x = lax.axis_index("xl")
    place = lax.axis_index("y")
    core = lax.axis_index("core")
    stage = high_x + 2 * low_x
    rows = weights.shape[2]

    own = lax.dynamic_index_in_dim(weights, low_x, 0, keepdims=False)[0]
    partner_own = lax.dynamic_index_in_dim(weights, 1 - low_x, 0, keepdims=False)[0]
    other = from_partner(partner_own)
    shard = jnp.where(low_x == 0, jnp.stack([own, other]), jnp.stack([other, own]))
    gathered = lax.all_gather(shard, ("y", "z", "core"), axis=0, tiled=False)
    gathered = gathered.reshape(LAYERS, 8, 2, 2, rows, WIDTH)

    pick = lambda v: lax.dynamic_slice_in_dim(v, 2 * place, 2, 0)
    tokens = 4 * PATCH
    x = both_halves(pick(patches).reshape(2 * PATCH, D), low_x).reshape(tokens, D)
    g = both_halves(pick(cotangent).reshape(2 * PATCH, D), low_x).reshape(tokens, D)
    span = both_halves(pick(lengths).astype(F32), low_x).reshape(4, PATCH).astype(jnp.int32)
    cosine, sine = rotary_tables(span)

    stored = []
    for turn in range(LAYERS - 1):
        flag = (stage == turn).astype(jnp.int32).reshape(1)
        if turn > 0:
            x = lax.ppermute(x, ("xh", "xl"), [(STAGE_X[turn - 1], STAGE_X[turn])])
        x, *stored = run_forward(flag, x, cosine, sine, gathered, stored)
    inputs, normed, *shared = stored

    x = lax.ppermute(x, ("xh", "xl"), [(STAGE_X[LAYERS - 2], STAGE_X[LAYERS - 1])])
    flag = (stage == LAYERS - 1).astype(jnp.int32).reshape(1)
    g, normed, grads = run_turn(flag, x, g, cosine, sine, gathered, normed)
    grads = [grads]
    g, late = lax.optimization_barrier((g, gathered))
    top = ordered(late, LAYERS - 1)
    for turn in reversed(range(LAYERS - 1)):
        flag = (stage == turn).astype(jnp.int32).reshape(1)
        g = lax.ppermute(g, ("xh", "xl"), [(STAGE_X[turn + 1], STAGE_X[turn])])
        g, *grads = run_backward(flag, g, cosine, sine, top, gathered, [inputs, *shared], grads)
    grads = grads[0]

    normed_rows = jnp.concatenate(spread_over_y(normed, place))
    sibling = lambda v: lax.ppermute(v, "core", ring(2, 1))
    normed_rows = jnp.concatenate([normed_rows, sibling(normed_rows)])
    half = WIDTH // 2
    grad_rows = jnp.concatenate(spread_over_y(grads, place))
    mine = lax.dynamic_slice_in_dim(grad_rows, core * half, half, 1)
    sent = lax.dynamic_slice_in_dim(grad_rows, (1 - core) * half, half, 1)
    grad_rows = jnp.concatenate([mine, sibling(sent)])
    terms = dot(normed_rows, grad_rows, 0, 0).astype(BF16)
    total = lax.psum_scatter(terms, "z", scatter_dimension=0, tiled=True)
    total = total.reshape(2, 2, rows, half)

    def block(low, row_core):
        return lax.dynamic_slice(total, (low, row_core, 0, 0), (1, 1, rows, half))[0, 0]

    came = [[block(low_x, core), None], [None, None]]
    for far in range(2):
        for beside in range(2):
            if far or beside:
                pairs = [(i, i ^ (2 * far + beside)) for i in range(4)]
                came[far][beside] = lax.ppermute(
                    block(low_x ^ far, core ^ beside), ("xl", "core"), pairs
                )

    def source(low, col):
        same_core = [jnp.where(core == col, came[far][0], came[far][1]) for far in range(2)]
        return jnp.where(low_x == low, same_core[0], same_core[1])

    result = jnp.stack(
        [jnp.concatenate([source(low, col) for col in range(2)], axis=1) for low in range(2)]
    )
    return result.astype(F32)[:, None]


def solution(mesh):
    fine = Mesh(mesh.devices.reshape(2, 4, 8, 2, 2), ("xh", "y", "z", "xl", "core"))
    dp = ("z", "xl", "core")
    return jax.shard_map(
        local,
        mesh=fine,
        in_specs=(
            P(dp, None, None),
            P(dp, None),
            P(dp, None, None),
            P(None, ("xh", "y"), dp, None),
        ),
        out_specs=P(None, ("xh", "y"), dp, None),
        check_vma=False,
    )
```

```python
import jax
import jax.numpy as jnp
from jax import lax
from jax.experimental import pallas as pl
from jax.experimental.pallas import tpu as pltpu
from jax.sharding import Mesh, PartitionSpec as P

D = 2048
HEADS = 16
KV_HEADS = 4
GROUP = HEADS // KV_HEADS
QK_DIM = 64
V_DIM = 128
PATCH = 16
QUERY_WIDTH = HEADS * QK_DIM
KEY_WIDTH = KV_HEADS * QK_DIM
VALUE_START = QUERY_WIDTH + KEY_WIDTH
WIDTH = VALUE_START + KV_HEADS * V_DIM
ROPE_BASE = 500000.0
EPSILON = 1e-05
LAYERS = 4
LANES = 128
COLUMNS = 256
STAGE_X = (0, 2, 1, 3)
F32 = jnp.float32
BF16 = jnp.bfloat16


def dot(a, b, a_dim, b_dim):
    return lax.dot_general(
        a, b, (((a_dim,), (b_dim,)), ((), ())), preferred_element_type=F32
    )


def lane_index(rows):
    return lax.broadcasted_iota(jnp.int32, (rows, LANES), 1)


def swap_halves(chunk):
    lanes = lane_index(chunk.shape[0])
    ahead = pltpu.roll(chunk, LANES - QK_DIM // 2, 1)
    behind = pltpu.roll(chunk, QK_DIM // 2, 1)
    return jnp.where(lanes % QK_DIM < QK_DIM // 2, ahead, behind)


def score_mask(tokens):
    rows = lax.broadcasted_iota(jnp.int32, (GROUP * tokens, tokens), 0) % tokens
    columns = lax.broadcasted_iota(jnp.int32, (GROUP * tokens, tokens), 1)
    return (rows // PATCH == columns // PATCH) & (columns <= rows)


def rotated_chunk(qkv, index, cosine, sine):
    chunk = qkv[:, index * LANES : (index + 1) * LANES]
    return chunk * cosine + swap_halves(chunk) * sine


def group_parts(qkv, group, cosine, sine):
    low = lane_index(qkv.shape[0]) < QK_DIM
    rows = []
    for pair in range(2):
        chunk = rotated_chunk(qkv, 2 * group + pair, cosine, sine)
        rows.append(jnp.where(low, chunk, 0.0))
        rows.append(jnp.where(low, 0.0, chunk))
    queries = jnp.concatenate(rows, axis=0).astype(BF16)
    chunk = rotated_chunk(qkv, QUERY_WIDTH // LANES + group // 2, cosine, sine)
    other = pltpu.roll(chunk, QK_DIM, 1)
    keys_part = jnp.where(low, chunk, other) if group % 2 == 0 else jnp.where(low, other, chunk)
    values_part = qkv[:, VALUE_START + group * V_DIM : VALUE_START + (group + 1) * V_DIM]
    return queries, keys_part.astype(BF16), values_part.astype(BF16)


def group_probs(queries, keys_part, mask):
    scores = dot(queries, keys_part, 1, 1) * (1.0 / QK_DIM**0.5)
    raised = jnp.where(mask, jnp.exp(jnp.where(mask, scores, 0.0)), 0.0)
    return raised / jnp.sum(raised, axis=-1, keepdims=True)


def layer_copies(slot, layer, weights_ref, held, sems):
    return [pltpu.make_async_copy(weights_ref.at[layer], held.at[slot], sems.at[slot])]


def rows_in_order(pieces):
    return lambda count: jnp.concatenate(
        [pieces(z, core, low) for z in range(count) for low in range(2) for core in range(2)]
    )


def start_all(copies):
    for copy in copies:
        copy.start()


def wait_all(copies):
    for copy in copies:
        copy.wait()


COLUMN_STEPS = WIDTH // COLUMNS
ROW_STEPS = D // COLUMNS
SLOTS = LAYERS - 1


def forward_layer(
    layer, ready, block_of, cosine, sine, mask,
    inputs_ref, normed_ref, values_ref, queries_ref, keys_ref, probs_ref, target, qkv_ref,
):
    x = inputs_ref[layer]
    tokens = x.shape[0]
    wide = x.astype(F32)
    scale = lax.rsqrt(jnp.mean(wide * wide, axis=-1, keepdims=True) + EPSILON)
    normed = (wide * scale).astype(BF16)
    normed_ref[layer] = normed
    ready()
    for step in range(COLUMN_STEPS):
        columns = slice(step * COLUMNS, (step + 1) * COLUMNS)
        block = rows_in_order(lambda z, core, low: block_of(z, core, low, columns))(8)
        qkv_ref[:, columns] = dot(normed, block, 1, 0).astype(BF16)
    qkv = qkv_ref[...].astype(F32)
    values_ref[layer] = qkv_ref[:, VALUE_START:]
    for group in range(KV_HEADS):
        queries, keys_part, values_part = group_parts(qkv, group, cosine, sine)
        probs = group_probs(queries, keys_part, mask)
        queries_ref[layer, group] = queries
        keys_ref[layer, group] = keys_part
        probs_ref[layer, group] = probs
        mixed = dot(probs.astype(BF16), values_part, 1, 0)
        for r in range(GROUP):
            head = group * GROUP + r
            span = slice(head * V_DIM, (head + 1) * V_DIM)
            value = inputs_ref[layer, :, span].astype(F32) + mixed[r * tokens : (r + 1) * tokens]
            target(span, value.astype(BF16))


def store_copies(layer, local_refs, outer_refs, sems, inward):
    copies = []
    for index, (inner, outer) in enumerate(zip(local_refs, outer_refs)):
        ends = (outer.at[layer], inner.at[layer]) if inward else (inner.at[layer], outer.at[layer])
        copies.append(pltpu.make_async_copy(*ends, sems.at[layer, index]))
    return copies


def forward_stage(
    x_ref, cosine_ref, sine_ref, weights_ref, stores, outs, held, qkv_ref, sems, out_sems, leave
):
    inputs_ref = stores[0]
    for layer in range(LAYERS):
        start_all(layer_copies(layer, layer, weights_ref, held, sems))
    inputs_ref[0] = x_ref[...]
    cosine = cosine_ref[...]
    sine = sine_ref[...]
    mask = score_mask(x_ref.shape[0])

    def run(layer, target):
        forward_layer(
            layer,
            lambda: wait_all(layer_copies(layer, layer, weights_ref, held, sems)),
            lambda z, core, low, columns: held[layer, z, core, low, :, columns],
            cosine, sine, mask, *stores, target, qkv_ref,
        )
        start_all(store_copies(layer, stores[: len(outs)], outs, out_sems, False))

    def body(layer, carry):
        def target(span, value):
            inputs_ref[layer + 1, :, span] = value

        run(layer, target)
        return carry

    lax.fori_loop(0, LAYERS - 1, body, 0)
    run(LAYERS - 1, leave)


def forward_kernel(flag_ref, x_ref, cosine_ref, sine_ref, weights_ref, *rest):
    held, qkv_ref, *stores, sems, out_sems = rest[-10:]
    last_ref, *outs = rest[-17:-10]

    @pl.when(flag_ref[0] == 1)
    def active():
        def leave(span, value):
            last_ref[:, span] = value

        forward_stage(
            x_ref, cosine_ref, sine_ref, weights_ref, stores, outs, held, qkv_ref, sems,
            out_sems, leave,
        )
        for layer in range(LAYERS):
            wait_all(store_copies(layer, stores, outs, out_sems, False))


def turn_kernel(flag_ref, x_ref, g_ref, cosine_ref, sine_ref, weights_ref, _normed, *rest):
    first_ref, normed_out, grad_out, held, qkv_ref, *stores = rest[:-4]
    grad_ref, sems, out_sems, grad_sems = rest[-4:]
    normed_ref, inputs_ref, *shared = stores

    @pl.when(flag_ref[0] == 1)
    def active():
        def leave(span, value):
            first_ref[:, span] = value

        forward_stage(
            x_ref, cosine_ref, sine_ref, weights_ref, [inputs_ref, normed_ref, *shared], [],
            held, qkv_ref, sems, out_sems, leave,
        )
        for layer in range(LAYERS):
            start_all(store_copies(layer, [normed_ref], [normed_out], out_sems, False))
        first_ref[...] = g_ref[...]

        def body(step, carry):
            layer = LAYERS - 1 - step
            backward_layer(
                layer, lambda: None, lambda z, core, low: held[layer, z, core, low], cosine_ref, sine_ref,
                inputs_ref, *shared, first_ref, grad_ref,
            )
            start_all(store_copies(layer, [grad_ref], [grad_out], grad_sems, False))
            return carry

        lax.fori_loop(0, LAYERS, body, 0)
        for layer in range(LAYERS):
            wait_all(store_copies(layer, [normed_ref], [normed_out], out_sems, False))
            wait_all(store_copies(layer, [grad_ref], [grad_out], grad_sems, False))


def backward_layer(
    layer, ready, block_of, cosine_ref, sine_ref, inputs_ref, values_ref, queries_ref,
    keys_ref, probs_ref, first_ref, grad_ref,
):
    upstream = first_ref[...]
    tokens = upstream.shape[0]
    cosine = cosine_ref[...]
    sine = sine_ref[...]
    low = lane_index(tokens) < QK_DIM
    key_grads = []
    for group in range(KV_HEADS):
        queries = queries_ref[layer, group]
        keys_part = keys_ref[layer, group]
        probs = probs_ref[layer, group]
        values_part = values_ref[layer, :, group * V_DIM : (group + 1) * V_DIM]
        rows = [
            upstream[:, (group * GROUP + r) * V_DIM : (group * GROUP + r + 1) * V_DIM]
            for r in range(GROUP)
        ]
        stacked = jnp.concatenate(rows, axis=0)
        grad_probs = dot(stacked, values_part, 1, 1)
        weighted = jnp.sum(probs * grad_probs, axis=-1, keepdims=True)
        grad_scores = (probs * (grad_probs - weighted) * (1.0 / QK_DIM**0.5)).astype(BF16)
        grad_values = dot(probs.astype(BF16), stacked, 0, 0)
        grad_ref[layer, :, VALUE_START + group * V_DIM : VALUE_START + (group + 1) * V_DIM] = (
            grad_values.astype(BF16)
        )
        grad_queries = dot(grad_scores, keys_part, 1, 0)
        for pair in range(2):
            first = grad_queries[2 * pair * tokens : (2 * pair + 1) * tokens]
            second = grad_queries[(2 * pair + 1) * tokens : (2 * pair + 2) * tokens]
            chunk = jnp.where(low, first, second)
            chunk = chunk * cosine - swap_halves(chunk) * sine
            start_at = (2 * group + pair) * LANES
            grad_ref[layer, :, start_at : start_at + LANES] = chunk.astype(BF16)
        halves = dot(grad_scores, queries, 0, 0)
        key_grads.append(halves + pltpu.roll(halves, QK_DIM, 1))
    for pair in range(2):
        chunk = jnp.where(low, key_grads[2 * pair], key_grads[2 * pair + 1])
        chunk = chunk * cosine - swap_halves(chunk) * sine
        start_at = QUERY_WIDTH + pair * LANES
        grad_ref[layer, :, start_at : start_at + LANES] = chunk.astype(BF16)
    grad_qkv = grad_ref[layer]
    wide = inputs_ref[layer].astype(F32)
    parts = []
    ready()
    for step in range(ROW_STEPS):
        block = rows_in_order(lambda z, core, low: block_of(step, core, low))(1)
        parts.append(dot(grad_qkv, block, 1, 1))
    grad_normed = jnp.concatenate(parts, axis=1)
    scale = lax.rsqrt(jnp.mean(wide * wide, axis=-1, keepdims=True) + EPSILON)
    inner = jnp.mean(grad_normed * wide, axis=-1, keepdims=True)
    grad_inputs = scale * grad_normed - wide * (scale * scale * scale * inner)
    first_ref[...] = (upstream.astype(F32) + grad_inputs).astype(BF16)


def backward_kernel(flag_ref, g_ref, cosine_ref, sine_ref, *rest):
    layer_refs = rest[:LAYERS]
    outer = rest[LAYERS : LAYERS + 5]
    first_ref, grad_out, *stores, grad_ref, in_sems, out_sems = rest[-10:]

    @pl.when(flag_ref[0] == 1)
    def active():
        for layer in reversed(range(LAYERS)):
            start_all(store_copies(layer, stores, outer, in_sems, True))
        first_ref[...] = g_ref[...]
        for layer in reversed(range(LAYERS)):
            held = layer_refs[layer]
            wait_all(store_copies(layer, stores, outer, in_sems, True))
            backward_layer(
                layer, lambda: None, lambda z, core, low, held=held: held[z, core, low],
                cosine_ref, sine_ref, *stores, first_ref, grad_ref,
            )
            start_all(store_copies(layer, [grad_ref], [grad_out], out_sems, False))
        for layer in range(LAYERS):
            wait_all(store_copies(layer, [grad_ref], [grad_out], out_sems, False))


VMEM_SPEC = pl.BlockSpec(memory_space=pltpu.VMEM)
SMEM_SPEC = pl.BlockSpec(memory_space=pltpu.SMEM)
HBM_SPEC = pl.BlockSpec(memory_space=pltpu.HBM)


def stage_params(limit):
    return pltpu.CompilerParams(vmem_limit_bytes=limit * 1024 * 1024)


def stage_cost(tokens):
    return pl.CostEstimate(
        flops=2 * LAYERS * tokens * D * WIDTH,
        bytes_accessed=2 * LAYERS * D * WIDTH,
        transcendentals=0,
    )


def buffers(shapes):
    return [pltpu.VMEM(each.shape, each.dtype) for each in shapes]


def held_scratch(slots):
    return pltpu.VMEM((slots, 8, 2, 2, 64, WIDTH), BF16)


def weight_sems(slots):
    return pltpu.SemaphoreType.DMA((slots,))


def copy_sems(count):
    return pltpu.SemaphoreType.DMA((LAYERS, count))


def store_shapes(tokens):
    return [
        jax.ShapeDtypeStruct((LAYERS, tokens, D), BF16),
        jax.ShapeDtypeStruct((LAYERS, tokens, D), BF16),
        jax.ShapeDtypeStruct((LAYERS, tokens, KV_HEADS * V_DIM), BF16),
        jax.ShapeDtypeStruct((LAYERS, KV_HEADS, GROUP * tokens, LANES), BF16),
        jax.ShapeDtypeStruct((LAYERS, KV_HEADS, tokens, LANES), BF16),
        jax.ShapeDtypeStruct((LAYERS, KV_HEADS, GROUP * tokens, tokens), F32),
    ]


def in_hbm(value):
    return pltpu.with_memory_space_constraint(value, pltpu.HBM)


def in_hbm_shape(shape):
    return pltpu.HBM(shape.shape, shape.dtype)


def grad_shape(tokens):
    return jax.ShapeDtypeStruct((LAYERS, tokens, WIDTH), BF16)


def run_forward(flag, x, cosine, sine, weights, stored):
    tokens = x.shape[0]
    shapes = store_shapes(tokens)
    return pl.pallas_call(
        forward_kernel,
        in_specs=[SMEM_SPEC] + [VMEM_SPEC] * 3 + [HBM_SPEC] * (1 + len(stored)),
        out_specs=[VMEM_SPEC] + [HBM_SPEC] * len(shapes),
        out_shape=[jax.ShapeDtypeStruct((tokens, D), BF16), *map(in_hbm_shape, shapes)],
        input_output_aliases={5 + i: 1 + i for i in range(len(stored))},
        scratch_shapes=[
            held_scratch(LAYERS),
            pltpu.VMEM((tokens, WIDTH), BF16),
            *buffers(shapes),
            weight_sems(LAYERS),
            copy_sems(len(shapes)),
        ],
        cost_estimate=stage_cost(tokens),
        name="forward_stage",
        compiler_params=stage_params(40),
    )(flag, x, cosine, sine, *map(in_hbm, [weights, *stored]))


def run_turn(flag, x, g, cosine, sine, weights, normed):
    tokens = g.shape[0]
    shapes = store_shapes(tokens)
    return pl.pallas_call(
        turn_kernel,
        in_specs=[SMEM_SPEC] + [VMEM_SPEC] * 4 + [HBM_SPEC] * 2,
        out_specs=[VMEM_SPEC] + [HBM_SPEC] * 2,
        out_shape=[
            jax.ShapeDtypeStruct((tokens, D), BF16),
            in_hbm_shape(shapes[1]),
            in_hbm_shape(grad_shape(tokens)),
        ],
        input_output_aliases={6: 1},
        scratch_shapes=[
            held_scratch(LAYERS),
            pltpu.VMEM((tokens, WIDTH), BF16),
            *buffers([shapes[1], shapes[0], *shapes[2:]]),
            pltpu.VMEM((LAYERS, tokens, WIDTH), BF16),
            weight_sems(LAYERS),
            copy_sems(1),
            copy_sems(1),
        ],
        cost_estimate=stage_cost(tokens),
        name="turn_stage",
        compiler_params=stage_params(42),
    )(flag, x, g, cosine, sine, *map(in_hbm, [weights, normed]))


def run_backward(flag, g, cosine, sine, weights, stored, grads):
    tokens = g.shape[0]
    shapes = store_shapes(tokens)
    return pl.pallas_call(
        backward_kernel,
        in_specs=[SMEM_SPEC] + [VMEM_SPEC] * (3 + LAYERS) + [HBM_SPEC] * (5 + len(grads)),
        out_specs=[VMEM_SPEC, HBM_SPEC],
        out_shape=[jax.ShapeDtypeStruct((tokens, D), BF16), in_hbm_shape(grad_shape(tokens))],
        input_output_aliases={9 + LAYERS: 1},
        scratch_shapes=[
            *buffers([shapes[0], *shapes[2:], grad_shape(tokens)]),
            copy_sems(5),
            copy_sems(1),
        ],
        cost_estimate=stage_cost(tokens),
        name="backward_stage",
        compiler_params=stage_params(12),
    )(flag, g, cosine, sine, *weights, *map(in_hbm, [*stored, *grads]))


def ring(size, by):
    return [(i, (i + by) % size) for i in range(size)]


def from_partner(value):
    return lax.ppermute(value, "xl", ring(2, 1))


def both_halves(value, low_x):
    other = from_partner(value)
    return jnp.where(low_x == 0, jnp.stack([value, other]), jnp.stack([other, value]))


def rotary_tables(lengths):
    half = QK_DIM // 2
    starts = jnp.cumsum(lengths, axis=-1) - lengths
    freqs = ROPE_BASE ** (-jnp.arange(half, dtype=F32) * 2.0 / (2 * half))
    angles = starts.astype(F32).reshape(-1, 1) * freqs
    cosine, sine = jnp.cos(angles), jnp.sin(angles)
    return (
        jnp.concatenate([cosine] * 4, axis=1),
        jnp.concatenate([-sine, sine, -sine, sine], axis=1),
    )


def spread_over_y(value, place):
    pieces = [lax.dynamic_index_in_dim(value, place, 0, keepdims=False)]
    for by in (1, 3, 2):
        piece = lax.dynamic_index_in_dim(value, (place + by) % 4, 0, keepdims=False)
        pieces.append(lax.ppermute(piece, "y", ring(4, by)))
    return pieces


def local(patches, lengths, cotangent, weights):
    high_x = lax.axis_index("xh")
    low_x = lax.axis_index("xl")
    place = lax.axis_index("y")
    core = lax.axis_index("core")
    stage = high_x + 2 * low_x
    rows = weights.shape[2]

    own = lax.dynamic_index_in_dim(weights, low_x, 0, keepdims=False)[0]
    partner_own = lax.dynamic_index_in_dim(weights, 1 - low_x, 0, keepdims=False)[0]
    other = from_partner(partner_own)
    shard = jnp.where(low_x == 0, jnp.stack([own, other]), jnp.stack([other, own]))
    gathered = lax.all_gather(shard, ("y", "z", "core"), axis=0, tiled=False)
    gathered = gathered.reshape(LAYERS, 8, 2, 2, rows, WIDTH)

    pick = lambda v: lax.dynamic_slice_in_dim(v, 2 * place, 2, 0)
    tokens = 4 * PATCH
    x = both_halves(pick(patches).reshape(2 * PATCH, D), low_x).reshape(tokens, D)
    g = both_halves(pick(cotangent).reshape(2 * PATCH, D), low_x).reshape(tokens, D)
    span = both_halves(pick(lengths).astype(F32), low_x).reshape(4, PATCH).astype(jnp.int32)
    cosine, sine = rotary_tables(span)

    stored = []
    for turn in range(LAYERS - 1):
        flag = (stage == turn).astype(jnp.int32).reshape(1)
        if turn > 0:
            x = lax.ppermute(x, ("xh", "xl"), [(STAGE_X[turn - 1], STAGE_X[turn])])
        x, *stored = run_forward(flag, x, cosine, sine, gathered, stored)
    inputs, normed, *shared = stored

    x = lax.ppermute(x, ("xh", "xl"), [(STAGE_X[LAYERS - 2], STAGE_X[LAYERS - 1])])
    flag = (stage == LAYERS - 1).astype(jnp.int32).reshape(1)
    g, normed, grads = run_turn(flag, x, g, cosine, sine, gathered, normed)
    grads = [grads]
    g, late = lax.optimization_barrier((g, gathered))
    layers = [late[layer] for layer in range(LAYERS)]
    for turn in reversed(range(LAYERS - 1)):
        flag = (stage == turn).astype(jnp.int32).reshape(1)
        g = lax.ppermute(g, ("xh", "xl"), [(STAGE_X[turn + 1], STAGE_X[turn])])
        g, *grads = run_backward(flag, g, cosine, sine, layers, [inputs, *shared], grads)
    grads = grads[0]

    normed_rows = jnp.concatenate(spread_over_y(normed, place))
    sibling = lambda v: lax.ppermute(v, "core", ring(2, 1))
    normed_rows = jnp.concatenate([normed_rows, sibling(normed_rows)])
    half = WIDTH // 2
    grad_rows = jnp.concatenate(spread_over_y(grads, place))
    mine = lax.dynamic_slice_in_dim(grad_rows, core * half, half, 1)
    sent = lax.dynamic_slice_in_dim(grad_rows, (1 - core) * half, half, 1)
    grad_rows = jnp.concatenate([mine, sibling(sent)])
    terms = dot(normed_rows, grad_rows, 0, 0).astype(BF16)
    total = lax.psum_scatter(terms, "z", scatter_dimension=0, tiled=True)
    total = total.reshape(2, 2, rows, half)

    def block(low, row_core):
        return lax.dynamic_slice(total, (low, row_core, 0, 0), (1, 1, rows, half))[0, 0]

    came = [[block(low_x, core), None], [None, None]]
    for far in range(2):
        for beside in range(2):
            if far or beside:
                pairs = [(i, i ^ (2 * far + beside)) for i in range(4)]
                came[far][beside] = lax.ppermute(
                    block(low_x ^ far, core ^ beside), ("xl", "core"), pairs
                )

    def source(low, col):
        same_core = [jnp.where(core == col, came[far][0], came[far][1]) for far in range(2)]
        return jnp.where(low_x == low, same_core[0], same_core[1])

    result = jnp.stack(
        [jnp.concatenate([source(low, col) for col in range(2)], axis=1) for low in range(2)]
    )
    return result.astype(F32)[:, None]


def solution(mesh):
    fine = Mesh(mesh.devices.reshape(2, 4, 8, 2, 2), ("xh", "y", "z", "xl", "core"))
    dp = ("z", "xl", "core")
    return jax.shard_map(
        local,
        mesh=fine,
        in_specs=(
            P(dp, None, None),
            P(dp, None),
            P(dp, None, None),
            P(None, ("xh", "y"), dp, None),
        ),
        out_specs=P(None, ("xh", "y"), dp, None),
        check_vma=False,
    )
```

```python
import jax
import jax.numpy as jnp
from jax import lax
from jax.experimental import pallas as pl
from jax.experimental.pallas import tpu as pltpu
from jax.sharding import Mesh, PartitionSpec as P

D = 2048
HEADS = 16
KV_HEADS = 4
GROUP = HEADS // KV_HEADS
QK_DIM = 64
V_DIM = 128
PATCH = 16
QUERY_WIDTH = HEADS * QK_DIM
KEY_WIDTH = KV_HEADS * QK_DIM
VALUE_START = QUERY_WIDTH + KEY_WIDTH
WIDTH = VALUE_START + KV_HEADS * V_DIM
ROPE_BASE = 500000.0
EPSILON = 1e-05
LAYERS = 4
LANES = 128
COLUMNS = 256
STAGE_X = (0, 2, 1, 3)
F32 = jnp.float32
BF16 = jnp.bfloat16


def dot(a, b, a_dim, b_dim):
    return lax.dot_general(
        a, b, (((a_dim,), (b_dim,)), ((), ())), preferred_element_type=F32
    )


def lane_index(rows):
    return lax.broadcasted_iota(jnp.int32, (rows, LANES), 1)


def swap_halves(chunk):
    lanes = lane_index(chunk.shape[0])
    ahead = pltpu.roll(chunk, LANES - QK_DIM // 2, 1)
    behind = pltpu.roll(chunk, QK_DIM // 2, 1)
    return jnp.where(lanes % QK_DIM < QK_DIM // 2, ahead, behind)


def score_mask(tokens):
    rows = lax.broadcasted_iota(jnp.int32, (GROUP * tokens, tokens), 0) % tokens
    columns = lax.broadcasted_iota(jnp.int32, (GROUP * tokens, tokens), 1)
    return (rows // PATCH == columns // PATCH) & (columns <= rows)


def rotated_chunk(qkv, index, cosine, sine):
    chunk = qkv[:, index * LANES : (index + 1) * LANES]
    return chunk * cosine + swap_halves(chunk) * sine


def group_parts(qkv, group, cosine, sine):
    low = lane_index(qkv.shape[0]) < QK_DIM
    rows = []
    for pair in range(2):
        chunk = rotated_chunk(qkv, 2 * group + pair, cosine, sine)
        rows.append(jnp.where(low, chunk, 0.0))
        rows.append(jnp.where(low, 0.0, chunk))
    queries = jnp.concatenate(rows, axis=0).astype(BF16)
    chunk = rotated_chunk(qkv, QUERY_WIDTH // LANES + group // 2, cosine, sine)
    other = pltpu.roll(chunk, QK_DIM, 1)
    keys_part = jnp.where(low, chunk, other) if group % 2 == 0 else jnp.where(low, other, chunk)
    values_part = qkv[:, VALUE_START + group * V_DIM : VALUE_START + (group + 1) * V_DIM]
    return queries, keys_part.astype(BF16), values_part.astype(BF16)


def group_probs(queries, keys_part, mask):
    scores = dot(queries, keys_part, 1, 1) * (1.0 / QK_DIM**0.5)
    raised = jnp.where(mask, jnp.exp(jnp.where(mask, scores, 0.0)), 0.0)
    return raised / jnp.sum(raised, axis=-1, keepdims=True)


def layer_copies(slot, layer, weights_ref, held, sems):
    return [pltpu.make_async_copy(weights_ref.at[layer], held.at[slot], sems.at[slot])]


def rows_in_order(pieces):
    return lambda count: jnp.concatenate(
        [pieces(z, core, low) for z in range(count) for low in range(2) for core in range(2)]
    )


def start_all(copies):
    for copy in copies:
        copy.start()


def wait_all(copies):
    for copy in copies:
        copy.wait()


COLUMN_STEPS = WIDTH // COLUMNS
ROW_STEPS = D // COLUMNS
SLOTS = LAYERS - 1


def forward_layer(
    layer, ready, block_of, cosine, sine, mask,
    inputs_ref, normed_ref, values_ref, queries_ref, keys_ref, probs_ref, target, qkv_ref,
):
    x = inputs_ref[layer]
    tokens = x.shape[0]
    wide = x.astype(F32)
    scale = lax.rsqrt(jnp.mean(wide * wide, axis=-1, keepdims=True) + EPSILON)
    normed = (wide * scale).astype(BF16)
    normed_ref[layer] = normed
    ready()
    for step in range(COLUMN_STEPS):
        columns = slice(step * COLUMNS, (step + 1) * COLUMNS)
        block = rows_in_order(lambda z, core, low: block_of(z, core, low, columns))(8)
        qkv_ref[:, columns] = dot(normed, block, 1, 0).astype(BF16)
    qkv = qkv_ref[...].astype(F32)
    values_ref[layer] = qkv_ref[:, VALUE_START:]
    for group in range(KV_HEADS):
        queries, keys_part, values_part = group_parts(qkv, group, cosine, sine)
        probs = group_probs(queries, keys_part, mask)
        queries_ref[layer, group] = queries
        keys_ref[layer, group] = keys_part
        probs_ref[layer, group] = probs
        mixed = dot(probs.astype(BF16), values_part, 1, 0)
        for r in range(GROUP):
            head = group * GROUP + r
            span = slice(head * V_DIM, (head + 1) * V_DIM)
            value = inputs_ref[layer, :, span].astype(F32) + mixed[r * tokens : (r + 1) * tokens]
            target(span, value.astype(BF16))


def store_copies(layer, local_refs, outer_refs, sems, inward):
    copies = []
    for index, (inner, outer) in enumerate(zip(local_refs, outer_refs)):
        ends = (outer.at[layer], inner.at[layer]) if inward else (inner.at[layer], outer.at[layer])
        copies.append(pltpu.make_async_copy(*ends, sems.at[layer, index]))
    return copies


def forward_stage(
    x_ref, cosine_ref, sine_ref, weights_ref, stores, outs, held, qkv_ref, sems, out_sems, leave
):
    inputs_ref = stores[0]
    for layer in range(LAYERS):
        start_all(layer_copies(layer, layer, weights_ref, held, sems))
    inputs_ref[0] = x_ref[...]
    cosine = cosine_ref[...]
    sine = sine_ref[...]
    mask = score_mask(x_ref.shape[0])

    def run(layer, target):
        forward_layer(
            layer,
            lambda: wait_all(layer_copies(layer, layer, weights_ref, held, sems)),
            lambda z, core, low, columns: held[layer, z, core, low, :, columns],
            cosine, sine, mask, *stores, target, qkv_ref,
        )
        start_all(store_copies(layer, stores[: len(outs)], outs, out_sems, False))

    def body(layer, carry):
        def target(span, value):
            inputs_ref[layer + 1, :, span] = value

        run(layer, target)
        return carry

    lax.fori_loop(0, LAYERS - 1, body, 0)
    run(LAYERS - 1, leave)


def forward_kernel(flag_ref, x_ref, cosine_ref, sine_ref, weights_ref, *rest):
    held, qkv_ref, *stores, sems, out_sems = rest[-10:]
    last_ref, *outs = rest[-17:-10]

    @pl.when(flag_ref[0] == 1)
    def active():
        def leave(span, value):
            last_ref[:, span] = value

        forward_stage(
            x_ref, cosine_ref, sine_ref, weights_ref, stores, outs, held, qkv_ref, sems,
            out_sems, leave,
        )
        for layer in range(LAYERS):
            wait_all(store_copies(layer, stores, outs, out_sems, False))


def turn_kernel(flag_ref, x_ref, g_ref, cosine_ref, sine_ref, weights_ref, _normed, *rest):
    first_ref, normed_out, grad_out, held, qkv_ref, *stores = rest[:-4]
    grad_ref, sems, out_sems, grad_sems = rest[-4:]
    normed_ref, inputs_ref, *shared = stores

    @pl.when(flag_ref[0] == 1)
    def active():
        def leave(span, value):
            first_ref[:, span] = value

        forward_stage(
            x_ref, cosine_ref, sine_ref, weights_ref, [inputs_ref, normed_ref, *shared], [],
            held, qkv_ref, sems, out_sems, leave,
        )
        for layer in range(LAYERS):
            start_all(store_copies(layer, [normed_ref], [normed_out], out_sems, False))
        first_ref[...] = g_ref[...]

        def body(step, carry):
            layer = LAYERS - 1 - step
            backward_layer(
                layer, lambda: None, lambda z, core, low: held[layer, z, core, low], cosine_ref, sine_ref,
                inputs_ref, *shared, first_ref, grad_ref,
            )
            start_all(store_copies(layer, [grad_ref], [grad_out], grad_sems, False))
            return carry

        lax.fori_loop(0, LAYERS, body, 0)
        for layer in range(LAYERS):
            wait_all(store_copies(layer, [normed_ref], [normed_out], out_sems, False))
            wait_all(store_copies(layer, [grad_ref], [grad_out], grad_sems, False))


def backward_layer(
    layer, ready, block_of, cosine_ref, sine_ref, inputs_ref, values_ref, queries_ref,
    keys_ref, probs_ref, first_ref, grad_ref,
):
    upstream = first_ref[...]
    tokens = upstream.shape[0]
    cosine = cosine_ref[...]
    sine = sine_ref[...]
    low = lane_index(tokens) < QK_DIM
    key_grads = []
    for group in range(KV_HEADS):
        queries = queries_ref[layer, group]
        keys_part = keys_ref[layer, group]
        probs = probs_ref[layer, group]
        values_part = values_ref[layer, :, group * V_DIM : (group + 1) * V_DIM]
        rows = [
            upstream[:, (group * GROUP + r) * V_DIM : (group * GROUP + r + 1) * V_DIM]
            for r in range(GROUP)
        ]
        stacked = jnp.concatenate(rows, axis=0)
        grad_probs = dot(stacked, values_part, 1, 1)
        weighted = jnp.sum(probs * grad_probs, axis=-1, keepdims=True)
        grad_scores = (probs * (grad_probs - weighted) * (1.0 / QK_DIM**0.5)).astype(BF16)
        grad_values = dot(probs.astype(BF16), stacked, 0, 0)
        grad_ref[layer, :, VALUE_START + group * V_DIM : VALUE_START + (group + 1) * V_DIM] = (
            grad_values.astype(BF16)
        )
        grad_queries = dot(grad_scores, keys_part, 1, 0)
        for pair in range(2):
            first = grad_queries[2 * pair * tokens : (2 * pair + 1) * tokens]
            second = grad_queries[(2 * pair + 1) * tokens : (2 * pair + 2) * tokens]
            chunk = jnp.where(low, first, second)
            chunk = chunk * cosine - swap_halves(chunk) * sine
            start_at = (2 * group + pair) * LANES
            grad_ref[layer, :, start_at : start_at + LANES] = chunk.astype(BF16)
        halves = dot(grad_scores, queries, 0, 0)
        key_grads.append(halves + pltpu.roll(halves, QK_DIM, 1))
    for pair in range(2):
        chunk = jnp.where(low, key_grads[2 * pair], key_grads[2 * pair + 1])
        chunk = chunk * cosine - swap_halves(chunk) * sine
        start_at = QUERY_WIDTH + pair * LANES
        grad_ref[layer, :, start_at : start_at + LANES] = chunk.astype(BF16)
    grad_qkv = grad_ref[layer]
    wide = inputs_ref[layer].astype(F32)
    parts = []
    ready()
    for step in range(ROW_STEPS):
        block = rows_in_order(lambda z, core, low: block_of(step, core, low))(1)
        parts.append(dot(grad_qkv, block, 1, 1))
    grad_normed = jnp.concatenate(parts, axis=1)
    scale = lax.rsqrt(jnp.mean(wide * wide, axis=-1, keepdims=True) + EPSILON)
    inner = jnp.mean(grad_normed * wide, axis=-1, keepdims=True)
    grad_inputs = scale * grad_normed - wide * (scale * scale * scale * inner)
    first_ref[...] = (upstream.astype(F32) + grad_inputs).astype(BF16)


def backward_kernel(flag_ref, g_ref, cosine_ref, sine_ref, *rest):
    layer_refs = rest[:LAYERS]
    outer = rest[LAYERS : LAYERS + 5]
    first_ref, grad_out, *stores, grad_ref, in_sems, out_sems = rest[-10:]

    @pl.when(flag_ref[0] == 1)
    def active():
        top = LAYERS - 1
        start_all(store_copies(top, stores, outer, in_sems, True))
        first_ref[...] = g_ref[...]
        for layer in reversed(range(LAYERS)):
            held = layer_refs[layer]
            wait_all(store_copies(layer, stores, outer, in_sems, True))
            if layer > 0:
                start_all(store_copies(layer - 1, stores, outer, in_sems, True))
            backward_layer(
                layer, lambda: None, lambda z, core, low, held=held: held[z, core, low],
                cosine_ref, sine_ref, *stores, first_ref, grad_ref,
            )
            start_all(store_copies(layer, [grad_ref], [grad_out], out_sems, False))
        for layer in range(LAYERS):
            wait_all(store_copies(layer, [grad_ref], [grad_out], out_sems, False))


VMEM_SPEC = pl.BlockSpec(memory_space=pltpu.VMEM)
SMEM_SPEC = pl.BlockSpec(memory_space=pltpu.SMEM)
HBM_SPEC = pl.BlockSpec(memory_space=pltpu.HBM)


def stage_params(limit):
    return pltpu.CompilerParams(vmem_limit_bytes=limit * 1024 * 1024)


def stage_cost(tokens):
    return pl.CostEstimate(
        flops=2 * LAYERS * tokens * D * WIDTH,
        bytes_accessed=2 * LAYERS * D * WIDTH,
        transcendentals=0,
    )


def buffers(shapes):
    return [pltpu.VMEM(each.shape, each.dtype) for each in shapes]


def held_scratch(slots):
    return pltpu.VMEM((slots, 8, 2, 2, 64, WIDTH), BF16)


def weight_sems(slots):
    return pltpu.SemaphoreType.DMA((slots,))


def copy_sems(count):
    return pltpu.SemaphoreType.DMA((LAYERS, count))


def store_shapes(tokens):
    return [
        jax.ShapeDtypeStruct((LAYERS, tokens, D), BF16),
        jax.ShapeDtypeStruct((LAYERS, tokens, D), BF16),
        jax.ShapeDtypeStruct((LAYERS, tokens, KV_HEADS * V_DIM), BF16),
        jax.ShapeDtypeStruct((LAYERS, KV_HEADS, GROUP * tokens, LANES), BF16),
        jax.ShapeDtypeStruct((LAYERS, KV_HEADS, tokens, LANES), BF16),
        jax.ShapeDtypeStruct((LAYERS, KV_HEADS, GROUP * tokens, tokens), F32),
    ]


def in_hbm(value):
    return pltpu.with_memory_space_constraint(value, pltpu.HBM)


def in_hbm_shape(shape):
    return pltpu.HBM(shape.shape, shape.dtype)


def grad_shape(tokens):
    return jax.ShapeDtypeStruct((LAYERS, tokens, WIDTH), BF16)


def run_forward(flag, x, cosine, sine, weights, stored):
    tokens = x.shape[0]
    shapes = store_shapes(tokens)
    return pl.pallas_call(
        forward_kernel,
        in_specs=[SMEM_SPEC] + [VMEM_SPEC] * 3 + [HBM_SPEC] * (1 + len(stored)),
        out_specs=[VMEM_SPEC] + [HBM_SPEC] * len(shapes),
        out_shape=[jax.ShapeDtypeStruct((tokens, D), BF16), *map(in_hbm_shape, shapes)],
        input_output_aliases={5 + i: 1 + i for i in range(len(stored))},
        scratch_shapes=[
            held_scratch(LAYERS),
            pltpu.VMEM((tokens, WIDTH), BF16),
            *buffers(shapes),
            weight_sems(LAYERS),
            copy_sems(len(shapes)),
        ],
        cost_estimate=stage_cost(tokens),
        name="forward_stage",
        compiler_params=stage_params(40),
    )(flag, x, cosine, sine, *map(in_hbm, [weights, *stored]))


def run_turn(flag, x, g, cosine, sine, weights, normed):
    tokens = g.shape[0]
    shapes = store_shapes(tokens)
    return pl.pallas_call(
        turn_kernel,
        in_specs=[SMEM_SPEC] + [VMEM_SPEC] * 4 + [HBM_SPEC] * 2,
        out_specs=[VMEM_SPEC] + [HBM_SPEC] * 2,
        out_shape=[
            jax.ShapeDtypeStruct((tokens, D), BF16),
            in_hbm_shape(shapes[1]),
            in_hbm_shape(grad_shape(tokens)),
        ],
        input_output_aliases={6: 1},
        scratch_shapes=[
            held_scratch(LAYERS),
            pltpu.VMEM((tokens, WIDTH), BF16),
            *buffers([shapes[1], shapes[0], *shapes[2:]]),
            pltpu.VMEM((LAYERS, tokens, WIDTH), BF16),
            weight_sems(LAYERS),
            copy_sems(1),
            copy_sems(1),
        ],
        cost_estimate=stage_cost(tokens),
        name="turn_stage",
        compiler_params=stage_params(42),
    )(flag, x, g, cosine, sine, *map(in_hbm, [weights, normed]))


def run_backward(flag, g, cosine, sine, weights, stored, grads):
    tokens = g.shape[0]
    shapes = store_shapes(tokens)
    return pl.pallas_call(
        backward_kernel,
        in_specs=[SMEM_SPEC] + [VMEM_SPEC] * (3 + LAYERS) + [HBM_SPEC] * (5 + len(grads)),
        out_specs=[VMEM_SPEC, HBM_SPEC],
        out_shape=[jax.ShapeDtypeStruct((tokens, D), BF16), in_hbm_shape(grad_shape(tokens))],
        input_output_aliases={9 + LAYERS: 1},
        scratch_shapes=[
            *buffers([shapes[0], *shapes[2:], grad_shape(tokens)]),
            copy_sems(5),
            copy_sems(1),
        ],
        cost_estimate=stage_cost(tokens),
        name="backward_stage",
        compiler_params=stage_params(12),
    )(flag, g, cosine, sine, *weights, *map(in_hbm, [*stored, *grads]))


def ring(size, by):
    return [(i, (i + by) % size) for i in range(size)]


def from_partner(value):
    return lax.ppermute(value, "xl", ring(2, 1))


def both_halves(value, low_x):
    other = from_partner(value)
    return jnp.where(low_x == 0, jnp.stack([value, other]), jnp.stack([other, value]))


def rotary_tables(lengths):
    half = QK_DIM // 2
    starts = jnp.cumsum(lengths, axis=-1) - lengths
    freqs = ROPE_BASE ** (-jnp.arange(half, dtype=F32) * 2.0 / (2 * half))
    angles = starts.astype(F32).reshape(-1, 1) * freqs
    cosine, sine = jnp.cos(angles), jnp.sin(angles)
    return (
        jnp.concatenate([cosine] * 4, axis=1),
        jnp.concatenate([-sine, sine, -sine, sine], axis=1),
    )


def spread_over_y(value, place):
    pieces = [lax.dynamic_index_in_dim(value, place, 0, keepdims=False)]
    for by in (1, 3, 2):
        piece = lax.dynamic_index_in_dim(value, (place + by) % 4, 0, keepdims=False)
        pieces.append(lax.ppermute(piece, "y", ring(4, by)))
    return pieces


def local(patches, lengths, cotangent, weights):
    high_x = lax.axis_index("xh")
    low_x = lax.axis_index("xl")
    place = lax.axis_index("y")
    core = lax.axis_index("core")
    stage = high_x + 2 * low_x
    rows = weights.shape[2]

    own = lax.dynamic_index_in_dim(weights, low_x, 0, keepdims=False)[0]
    partner_own = lax.dynamic_index_in_dim(weights, 1 - low_x, 0, keepdims=False)[0]
    other = from_partner(partner_own)
    shard = jnp.where(low_x == 0, jnp.stack([own, other]), jnp.stack([other, own]))
    gathered = lax.all_gather(shard, ("y", "z", "core"), axis=0, tiled=False)
    gathered = gathered.reshape(LAYERS, 8, 2, 2, rows, WIDTH)

    pick = lambda v: lax.dynamic_slice_in_dim(v, 2 * place, 2, 0)
    tokens = 4 * PATCH
    x = both_halves(pick(patches).reshape(2 * PATCH, D), low_x).reshape(tokens, D)
    g = both_halves(pick(cotangent).reshape(2 * PATCH, D), low_x).reshape(tokens, D)
    span = both_halves(pick(lengths).astype(F32), low_x).reshape(4, PATCH).astype(jnp.int32)
    cosine, sine = rotary_tables(span)

    stored = []
    for turn in range(LAYERS - 1):
        flag = (stage == turn).astype(jnp.int32).reshape(1)
        if turn > 0:
            x = lax.ppermute(x, ("xh", "xl"), [(STAGE_X[turn - 1], STAGE_X[turn])])
        x, *stored = run_forward(flag, x, cosine, sine, gathered, stored)
    inputs, normed, *shared = stored

    x = lax.ppermute(x, ("xh", "xl"), [(STAGE_X[LAYERS - 2], STAGE_X[LAYERS - 1])])
    flag = (stage == LAYERS - 1).astype(jnp.int32).reshape(1)
    g, normed, grads = run_turn(flag, x, g, cosine, sine, gathered, normed)
    grads = [grads]
    g, late = lax.optimization_barrier((g, gathered))
    layers = [late[layer] for layer in range(LAYERS)]
    for turn in reversed(range(LAYERS - 1)):
        flag = (stage == turn).astype(jnp.int32).reshape(1)
        g = lax.ppermute(g, ("xh", "xl"), [(STAGE_X[turn + 1], STAGE_X[turn])])
        g, *grads = run_backward(flag, g, cosine, sine, layers, [inputs, *shared], grads)
    grads = grads[0]

    normed_rows = jnp.concatenate(spread_over_y(normed, place))
    sibling = lambda v: lax.ppermute(v, "core", ring(2, 1))
    normed_rows = jnp.concatenate([normed_rows, sibling(normed_rows)])
    half = WIDTH // 2
    grad_rows = jnp.concatenate(spread_over_y(grads, place))
    mine = lax.dynamic_slice_in_dim(grad_rows, core * half, half, 1)
    sent = lax.dynamic_slice_in_dim(grad_rows, (1 - core) * half, half, 1)
    grad_rows = jnp.concatenate([mine, sibling(sent)])
    terms = dot(normed_rows, grad_rows, 0, 0).astype(BF16)
    total = lax.psum_scatter(terms, "z", scatter_dimension=0, tiled=True)
    total = total.reshape(2, 2, rows, half)

    def block(low, row_core):
        return lax.dynamic_slice(total, (low, row_core, 0, 0), (1, 1, rows, half))[0, 0]

    came = [[block(low_x, core), None], [None, None]]
    for far in range(2):
        for beside in range(2):
            if far or beside:
                pairs = [(i, i ^ (2 * far + beside)) for i in range(4)]
                came[far][beside] = lax.ppermute(
                    block(low_x ^ far, core ^ beside), ("xl", "core"), pairs
                )

    def source(low, col):
        same_core = [jnp.where(core == col, came[far][0], came[far][1]) for far in range(2)]
        return jnp.where(low_x == low, same_core[0], same_core[1])

    result = jnp.stack(
        [jnp.concatenate([source(low, col) for col in range(2)], axis=1) for low in range(2)]
    )
    return result.astype(F32)[:, None]


def solution(mesh):
    fine = Mesh(mesh.devices.reshape(2, 4, 8, 2, 2), ("xh", "y", "z", "xl", "core"))
    dp = ("z", "xl", "core")
    return jax.shard_map(
        local,
        mesh=fine,
        in_specs=(
            P(dp, None, None),
            P(dp, None),
            P(dp, None, None),
            P(None, ("xh", "y"), dp, None),
        ),
        out_specs=P(None, ("xh", "y"), dp, None),
        check_vma=False,
    )
```
